256 devices in a mesh: pairs: 32 (over y, z), tm: 8 (over x, core).
Axes of the slice: x: 4, y: 4, z: 8, core: 2. Of those that a mesh axis runs over, the one named last changes fastest.
Arguments:
- spectra: bfloat16 [8, 256, 2, 32768], P('tm', 'pairs'), may hold values from -6 to 6
- channel_slot: int32 [256], P('pairs'), may hold values from 0 to 7, as said below
- tile_list: int32 [63, 2], replicated, may hold values from 0 to 31, as said below
- tile_owner: int32 [63], replicated, may hold values from 0 to 31, as said below
Outputs:
- correlations: float32 [128, 64, 256], P('pairs', 'tm')
The draws below stay inside these ranges and needn't reach their ends.
Inputs may be any that keep to these rules, and one draw needn't show every extreme that they name: `channel_slot`: within each block of 8 channels the values are a permutation of 0..7. `tile_list`: each row (i, j) has j = i or j = i + 1; every such pair of blocks appears exactly once, in some order. `tile_owner`: the owner of the tile in row p of tile_list is that row's i or i + 1; the tile of blocks 0 and 1 is owned by block 1; no owner holds more than 4 tiles, and some owner holds exactly 4.
All inputs are finite; a program needn't handle non-finite values.
Results may differ from the reference program's by a relative error of at most 0.00033.
Values may be sent and summed in bfloat16 or wider, within the bound.
A program may use at most 64 MiB of HBM per device.

```python
import math
import jax
import jax.numpy as jnp
from jax import lax

CH_DEV = 8
BINS = 32768
LAGS = 256
TILE_CAP = 4
WINDOWS = 8
CHANNELS = 256
N_PAIRS = 32


def banded_tiles(key):
    block_total = CHANNELS // CH_DEV
    tile_count = 2 * block_total - 1
    low_block = jnp.concatenate([jnp.arange(block_total, dtype=jnp.int32), jnp.arange(block_total - 1, dtype=jnp.int32)])
    high_block = jnp.concatenate([jnp.arange(block_total, dtype=jnp.int32), jnp.arange(1, block_total, dtype=jnp.int32)])
    owner_lift = jax.random.randint(jax.random.fold_in(key, 11), (tile_count,), 0, 2).astype(jnp.int32)
    owner_lift = jnp.where(low_block == block_total - 1, 0, owner_lift)
    owner_lift = jnp.where(low_block == 0, jnp.where(high_block == 1, 1, 0), owner_lift)
    busy_block = jax.random.randint(jax.random.fold_in(key, 12), (), 2, block_total - 1).astype(jnp.int32)
    owner_lift = jnp.where(low_block == busy_block - 1, 1, owner_lift)
    owner_lift = jnp.where(low_block == busy_block, 0, owner_lift)
    owner_map = (low_block + owner_lift).astype(jnp.int32)
    shuffle = jax.random.permutation(jax.random.fold_in(key, 13), tile_count)
    pairs_list = jnp.stack([low_block, high_block], axis=1)[shuffle]
    return (pairs_list.astype(jnp.int32), owner_map[shuffle].astype(jnp.int32))


def draw_tile_list(key, part):
    return banded_tiles(key)[0]


def draw_tile_owner(key, part):
    return banded_tiles(key)[1]


def draw_channel_slot(key, part):
    key = jax.random.fold_in(key, 5)
    block_keys = jax.random.split(key, CHANNELS // CH_DEV)
    permuted = jax.vmap(lambda block_key: jax.random.permutation(block_key, CH_DEV))(block_keys)
    return permuted.reshape(-1).astype(jnp.int32)


def steps_of(stream_key, shape, cuts, least, top_value):
    loudness = 1.0
    for position, parts in cuts:
        steps = jax.random.uniform(jax.random.fold_in(jax.random.fold_in(stream_key, 6), position), (parts,), jnp.float32, least / len(cuts), top_value / len(cuts))
        loudness = loudness * jnp.repeat(jnp.exp(steps), shape[position] // parts).reshape((-1,) + (1,) * (len(shape) - 1 - position))
    return loudness


def noise(stream_key, shape, deviation, most, cuts=(), kind=jnp.bfloat16):
    result = deviation * jax.random.normal(stream_key, shape, jnp.float32)
    if cuts:
        result = result * steps_of(stream_key, shape, cuts, -0.22, 0.18)
    return jnp.clip(result, -most, most).astype(kind)


def setup_inputs(seed: int = 0) -> dict:
    key_of = jax.random.split(jax.random.key(seed), 5)
    spectra = noise(key_of[0], (WINDOWS, CHANNELS, 2, BINS), 1.0, 6.0, ((0, 8), (1, 32)))
    channel_slot = draw_channel_slot(jax.random.fold_in(key_of[4], 71), 0)
    tile_list = draw_tile_list(jax.random.fold_in(key_of[4], 71), 0)
    tile_owner = draw_tile_owner(jax.random.fold_in(key_of[4], 71), 0)
    return {"spectra": spectra, "channel_slot": channel_slot, "tile_list": tile_list, "tile_owner": tile_owner}


def lag_table(freq_start, freq_width, bin_count, lag_count):
    freq_ids = freq_start + lax.iota(jnp.int32, freq_width)
    shift_lag = lax.iota(jnp.int32, lag_count) - lag_count // 2
    phase_steps = jnp.mod(freq_ids[:, None] * shift_lag[None, :], 2 * bin_count)
    phase_angle = phase_steps.astype(jnp.float32) * (math.pi / bin_count)
    cosine = jnp.cos(phase_angle).astype(jnp.bfloat16)
    sine_neg = (-jnp.sin(phase_angle)).astype(jnp.bfloat16)
    return jnp.concatenate([cosine, sine_neg], axis=0)

def cross_block(lead_block, tail_block):
    group_count = lead_block.shape[0]
    chan_count = lead_block.shape[1]
    lead_real = lead_block[:, :, 0].astype(jnp.float32)[:, :, None, :]
    lead_imag = lead_block[:, :, 1].astype(jnp.float32)[:, :, None, :]
    tail_real = tail_block[:, :, 0].astype(jnp.float32)[:, None, :, :]
    tail_imag = tail_block[:, :, 1].astype(jnp.float32)[:, None, :, :]
    real_part = lead_real * tail_real + lead_imag * tail_imag
    imag_part = lead_imag * tail_real - lead_real * tail_imag
    joined = jnp.concatenate([real_part.astype(jnp.bfloat16), imag_part.astype(jnp.bfloat16)], axis=-1)
    return joined.reshape(group_count, chan_count * chan_count, joined.shape[-1])

def reference(spectra, channel_slot, tile_list, tile_owner):
    block_base = lax.iota(jnp.int32, CHANNELS) // CH_DEV * CH_DEV
    ordered = jnp.take(spectra, (block_base + channel_slot).astype(jnp.int32), axis=1)
    lag_rows = lag_table(0, BINS, BINS, LAGS).astype(jnp.float32)
    norm_scale = 1.0 / math.sqrt(2.0 * BINS * WINDOWS)

    def one_tile(tile_row):
        lead_block = lax.dynamic_slice_in_dim(ordered, (tile_row[0] * CH_DEV).astype(jnp.int32), CH_DEV, 1)
        tail_block = lax.dynamic_slice_in_dim(ordered, (tile_row[1] * CH_DEV).astype(jnp.int32), CH_DEV, 1)
        cross_spec = cross_block(lead_block, tail_block)
        lagged = jnp.einsum('wpf,fl->wpl', cross_spec.astype(jnp.float32), lag_rows, precision=lax.Precision.HIGHEST)
        return lax.optimization_barrier(jnp.sum(lagged * norm_scale, axis=0))
    stacked = lax.map(one_tile, tile_list)
    tile_count = tile_list.shape[0]
    earlier = lax.iota(jnp.int32, tile_count)[:, None] > lax.iota(jnp.int32, tile_count)[None, :]
    slot_rank = lax.optimization_barrier(jnp.sum((tile_owner[:, None] == tile_owner[None, :]) & earlier, axis=1)).astype(jnp.int32)
    slot_index = (tile_owner * TILE_CAP + slot_rank).astype(jnp.int32)
    empty = jnp.zeros((N_PAIRS * TILE_CAP, CH_DEV * CH_DEV, LAGS), jnp.float32)
    return empty.at[slot_index].set(stacked)
```

```python
import functools
import math

import jax
import jax.numpy as jnp
import ml_dtypes
import numpy as np
from jax import lax
from jax.experimental import pallas as pl
from jax.experimental.pallas import tpu as pltpu
from jax.sharding import PartitionSpec as P

LAGS = 256
TILE_CAP = 4
CH = 8
HALF = LAGS // 2
TURN = 512
SHIFT = TURN // 4
STEP = 4096
MESH = pl.DeviceIdType.MESH
F32 = jnp.float32
BF16 = jnp.bfloat16


def lag_table(bins):
    bin_ids = np.arange(bins)
    turn_start = bin_ids // TURN * TURN
    moved = turn_start + (bin_ids - turn_start + SHIFT) % TURN

    def phase(ids, lags):
        steps = (ids[:, None] * lags[None, :]) % (2 * bins)
        return (steps.astype(np.float32) * np.float32(math.pi / bins)).astype(np.float64)

    cosine = np.cos(phase(bin_ids, np.arange(HALF)))
    sine = -np.sin(phase(moved, np.arange(HALF)))
    sine[:, :1] = np.cos(phase(bin_ids, np.array([HALF])))
    joined = np.concatenate([cosine, sine], axis=1)
    return joined.astype(np.float32).astype(ml_dtypes.bfloat16)


def moved_on(block):
    parts = []
    for start in range(0, block.shape[1], TURN):
        parts.append(block[:, start + SHIFT : start + TURN])
        parts.append(block[:, start : start + SHIFT])
    return jnp.concatenate(parts, axis=1)


def cross_rows(lead, tail):
    lead = lead.astype(F32)
    tail = tail.astype(F32)
    tail_re, tail_im = tail[:CH], tail[CH:]
    real, imag = [], []
    for a in range(CH):
        lead_re, lead_im = lead[a : a + 1], lead[CH + a : CH + a + 1]
        real.append(lead_re * tail_re + lead_im * tail_im)
        imag.append(lead_im * tail_re - lead_re * tail_im)
    real = jnp.concatenate(real, axis=0).astype(BF16)
    imag = jnp.concatenate(imag, axis=0).astype(BF16)
    return jnp.concatenate([real, moved_on(imag)], axis=0)


def folded(acc):
    real, imag = acc[: CH * CH, :], acc[CH * CH :, :]
    lane = lax.broadcasted_iota(jnp.int32, (CH * CH, HALF), 1)
    right = imag[:, HALF:] + jnp.where(lane == 0, real[:, HALF:], 0.0)
    return jnp.concatenate([real[:, :HALF], right], axis=1)


def kernel(
    n_pairs, n_tm, norm_scale,
    spectra, slot_hbm, tiles_hbm, owners_hbm, table_hbm,
    out,
    slot, tiles, owners, raw, own, from_right, from_left, table,
    diag_acc, low_acc, high_acc,
    diag_out, diag_in, side_out, side_in, hop_out, hop_in,
    index_sem, raw_sem, table_sem, send_sem, recv_sem, diag_send, diag_recv,
    side_send, side_recv, hop_send, hop_recv,
):
    bins = own.shape[1]
    half_bins = bins // 2
    steps = half_bins // STEP
    here = lax.axis_index("pairs")
    window = lax.axis_index("tm")
    right = (lax.rem(here + 1, n_pairs), window)
    left = (lax.rem(here + n_pairs - 1, n_pairs), window)

    def peer(k):
        return lax.rem(window + k, n_tm)

    barrier = pltpu.get_barrier_semaphore()
    for device in [right, left] + [(here, peer(k)) for k in range(1, n_tm)]:
        pl.semaphore_signal(barrier, inc=1, device_id=device, device_id_type=MESH)

    def lanes(index):
        return pl.ds(pl.multiple_of(index * STEP, STEP), STEP)

    order = [part for i in range(steps) for part in (i, steps + i)]

    def raw_copy(part):
        return pltpu.make_async_copy(
            spectra.at[:, :, lanes(part)], raw[part], raw_sem.at[part]
        )

    def table_copy(part):
        return pltpu.make_async_copy(
            table_hbm.at[lanes(part), :], table.at[lanes(part), :], table_sem.at[part]
        )

    index_copies = [
        pltpu.make_async_copy(source, target, index_sem.at[place])
        for place, (source, target) in enumerate(
            [(slot_hbm, slot), (tiles_hbm, tiles), (owners_hbm, owners)]
        )
    ]
    index_copies[0].start()
    for part in order:
        raw_copy(part).start()
    for copy in index_copies[1:]:
        copy.start()
    for part in range(2 * steps):
        table_copy(part).start()

    def low_copy(i):
        return pltpu.make_async_remote_copy(
            own.at[:, lanes(i)], from_right.at[:, lanes(i)],
            send_sem.at[i], recv_sem.at[i], device_id=left, device_id_type=MESH,
        )

    def high_copy(i):
        return pltpu.make_async_remote_copy(
            own.at[:, lanes(steps + i)], from_left.at[:, lanes(i)],
            send_sem.at[steps + i], recv_sem.at[steps + i],
            device_id=right, device_id_type=MESH,
        )

    def send(part):
        if part < steps:
            low_copy(part).start()
        else:
            high_copy(part - steps).start()

    index_copies[0].wait()
    rows = [slot[c] for c in range(CH)]
    for place, part in enumerate(order):
        raw_copy(part).wait()

        @pl.loop(0, STEP // 1024)
        def _(piece, part=part):
            offset = pl.multiple_of(piece * 1024, 1024)
            values = [raw[part][row, :, pl.ds(offset, 1024)].astype(F32) for row in rows]
            planar = [v[:1] for v in values] + [v[1:] for v in values]
            own[:, pl.ds(pl.multiple_of(part * STEP + offset, 1024), 1024)] = jnp.concatenate(planar, axis=0).astype(BF16)

        if place == steps - 1:
            pl.semaphore_wait(barrier, n_tm + 1)
            for earlier in order[: place + 1]:
                send(earlier)
        elif place >= steps:
            send(part)

    diag_acc[...] = jnp.zeros_like(diag_acc)
    low_acc[...] = jnp.zeros_like(low_acc)
    high_acc[...] = jnp.zeros_like(high_acc)

    @pl.loop(0, 2 * steps)
    def _(part):
        table_copy(part).wait()
        block = own[:, lanes(part)]
        diag_acc[...] += jnp.dot(
            cross_rows(block, block), table[lanes(part), :], preferred_element_type=F32
        )

    def diag_copy(k):
        return pltpu.make_async_remote_copy(
            diag_out.at[peer(k)], diag_in.at[k], diag_send.at[k], diag_recv.at[k],
            device_id=(here, peer(k)), device_id_type=MESH,
        )

    def side_copy(k):
        return pltpu.make_async_remote_copy(
            side_out.at[peer(k)], side_in.at[k], side_send.at[k], side_recv.at[k],
            device_id=(here, peer(k)), device_id_type=MESH,
        )

    diag = folded(diag_acc[...])
    for t in range(n_tm):
        diag_out[t] = diag[t * CH : (t + 1) * CH]
    for k in range(1, n_tm):
        diag_copy(k).start()

    for copy in index_copies[1:]:
        copy.wait()

    def next_tile(p, carry):
        count, kinds = carry[0], carry[1:]
        mine = owners[p] == here
        kind = 2 * (tiles[0, p] - here + 1) + tiles[1, p] - tiles[0, p]
        kinds = [
            jnp.where(mine & (count == s), kind, kinds[s]) for s in range(TILE_CAP)
        ]
        return (count + mine.astype(jnp.int32), *kinds)

    carry = (jnp.int32(0),) + (jnp.int32(-1),) * TILE_CAP
    kinds = lax.fori_loop(0, tiles.shape[1], next_tile, carry)[1:]

    @pl.loop(0, steps)
    def _(i):
        low_copy(i).wait_recv()
        low_acc[...] += jnp.dot(
            cross_rows(own[:, lanes(i)], from_right[:, lanes(i)]),
            table[lanes(i), :], preferred_element_type=F32,
        )
        high_copy(i).wait_recv()
        high_acc[...] += jnp.dot(
            cross_rows(from_left[:, lanes(i)], own[:, lanes(steps + i)]),
            table[lanes(steps + i), :], preferred_element_type=F32,
        )

    low, high = folded(low_acc[...]), folded(high_acc[...])
    for t in range(n_tm):
        side_out[t, :CH] = low[t * CH : (t + 1) * CH]
        side_out[t, CH:] = high[t * CH : (t + 1) * CH]
    for k in range(1, n_tm):
        side_copy(k).start()

    def right_copy(place):
        return pltpu.make_async_remote_copy(
            hop_out.at[place], hop_in.at[place], hop_send.at[place], hop_recv.at[place],
            device_id=right, device_id_type=MESH,
        )

    def left_copy(place):
        return pltpu.make_async_remote_copy(
            hop_out.at[place], hop_in.at[place], hop_send.at[place], hop_recv.at[place],
            device_id=left, device_id_type=MESH,
        )

    diag_sum = diag_out[window]
    for k in range(1, n_tm):
        diag_copy(k).wait_recv()
        diag_sum += diag_in[k]
    hop_out[0] = diag_sum
    right_copy(0).start()

    side_sum = side_out[window]
    for k in range(1, n_tm):
        side_copy(k).wait_recv()
        side_sum += side_in[k]
    hop_out[1] = side_sum[:CH]
    hop_out[2] = side_sum[CH:]
    right_copy(1).start()
    left_copy(2).start()

    right_copy(0).wait_recv()
    right_copy(1).wait_recv()
    left_copy(2).wait_recv()
    stacked = [hop_in[0], side_sum[CH:] + hop_in[1], diag_sum, side_sum[:CH] + hop_in[2]]
    lane = lax.broadcasted_iota(jnp.int32, (CH, HALF), 1)
    mirror = lax.rem(HALF - lane, HALF)
    for s in range(TILE_CAP):
        value = jnp.zeros((CH, LAGS), F32)
        for kind, tile in enumerate(stacked):
            value = jnp.where(kinds[s] == kind, tile, value)
        even, odd = value[:, :HALF], value[:, HALF:]
        before = jnp.where(lane == 0, odd, even - odd)
        before = jnp.take_along_axis(before, mirror, axis=1)
        after = jnp.where(lane == 0, even, even + odd)
        out[s] = jnp.concatenate([before, after], axis=1) * norm_scale

    for i in range(steps):
        low_copy(i).wait_send()
        high_copy(i).wait_send()
    for k in range(1, n_tm):
        diag_copy(k).wait_send()
        side_copy(k).wait_send()
    right_copy(0).wait_send()
    right_copy(1).wait_send()
    left_copy(2).wait_send()


def on_device(n_pairs, n_tm, spectra, channel_slot, tile_list, tile_owner):
    bins = spectra.shape[3]
    steps = bins // 2 // STEP
    dma = pltpu.SemaphoreType.DMA
    vmem = pl.BlockSpec(memory_space=pltpu.VMEM)
    hbm = pl.BlockSpec(memory_space=pl.ANY)
    return pl.pallas_call(
        functools.partial(kernel, n_pairs, n_tm, 1.0 / math.sqrt(2.0 * bins * n_tm)),
        out_shape=jax.ShapeDtypeStruct((TILE_CAP, CH, LAGS), F32),
        in_specs=[hbm] * 5,
        out_specs=vmem,
        scratch_shapes=[
            pltpu.SMEM(channel_slot.shape, jnp.int32),
            pltpu.SMEM(tile_list.shape[::-1], jnp.int32),
            pltpu.SMEM(tile_owner.shape, jnp.int32),
            [pltpu.VMEM((CH, 2, STEP), BF16) for _ in range(2 * steps)],
            pltpu.VMEM((2 * CH, bins), BF16),
            pltpu.VMEM((2 * CH, bins // 2), BF16),
            pltpu.VMEM((2 * CH, bins // 2), BF16),
            pltpu.VMEM((bins, LAGS), BF16),
            pltpu.VMEM((2 * CH * CH, LAGS), F32),
            pltpu.VMEM((2 * CH * CH, LAGS), F32),
            pltpu.VMEM((2 * CH * CH, LAGS), F32),
            pltpu.VMEM((n_tm, CH, LAGS), F32),
            pltpu.VMEM((n_tm, CH, LAGS), F32),
            pltpu.VMEM((n_tm, 2 * CH, LAGS), F32),
            pltpu.VMEM((n_tm, 2 * CH, LAGS), F32),
            pltpu.VMEM((3, CH, LAGS), F32),
            pltpu.VMEM((3, CH, LAGS), F32),
            dma((3,)),
            dma((2 * steps,)),
            dma((2 * steps,)),
            dma((2 * steps,)),
            dma((2 * steps,)),
            dma((n_tm,)),
            dma((n_tm,)),
            dma((n_tm,)),
            dma((n_tm,)),
            dma((3,)),
            dma((3,)),
        ],
        compiler_params=pltpu.CompilerParams(
            collective_id=0, has_side_effects=True, vmem_limit_bytes=63 * 1024 * 1024
        ),
    )(spectra[0], channel_slot, tile_list.T, tile_owner, jnp.asarray(lag_table(bins)))


def solution(mesh):
    placed = (P("tm", "pairs", None, None), P("pairs"), P(), P())
    body = functools.partial(on_device, mesh.shape["pairs"], mesh.shape["tm"])
    return jax.shard_map(
        body, mesh=mesh, in_specs=placed, out_specs=P("pairs", "tm", None), check_vma=False
    )
```

```python
import functools
import math

import jax
import jax.numpy as jnp
import ml_dtypes
import numpy as np
from jax import lax
from jax.experimental import pallas as pl
from jax.experimental.pallas import tpu as pltpu
from jax.sharding import PartitionSpec as P

LAGS = 256
TILE_CAP = 4
CH = 8
HALF = LAGS // 2
TURN = 512
SHIFT = TURN // 4
STEP = 4096
MESH = pl.DeviceIdType.MESH
F32 = jnp.float32
BF16 = jnp.bfloat16


def lag_table(bins):
    bin_ids = np.arange(bins)
    turn_start = bin_ids // TURN * TURN
    moved = turn_start + (bin_ids - turn_start + SHIFT) % TURN

    def phase(ids, lags):
        steps = (ids[:, None] * lags[None, :]) % (2 * bins)
        return (steps.astype(np.float32) * np.float32(math.pi / bins)).astype(np.float64)

    cosine = np.cos(phase(bin_ids, np.arange(HALF)))
    sine = -np.sin(phase(moved, np.arange(HALF)))
    sine[:, :1] = np.cos(phase(bin_ids, np.array([HALF])))
    joined = np.concatenate([cosine, sine], axis=1)
    return joined.astype(np.float32).astype(ml_dtypes.bfloat16)


def moved_on(block):
    parts = []
    for start in range(0, block.shape[1], TURN):
        parts.append(block[:, start + SHIFT : start + TURN])
        parts.append(block[:, start : start + SHIFT])
    return jnp.concatenate(parts, axis=1)


def cross_rows(lead, tail):
    lead = lead.astype(F32)
    tail = tail.astype(F32)
    tail_re, tail_im = tail[:CH], tail[CH:]
    real, imag = [], []
    for a in range(CH):
        lead_re, lead_im = lead[a : a + 1], lead[CH + a : CH + a + 1]
        real.append(lead_re * tail_re + lead_im * tail_im)
        imag.append(lead_im * tail_re - lead_re * tail_im)
    real = jnp.concatenate(real, axis=0).astype(BF16)
    imag = jnp.concatenate(imag, axis=0).astype(BF16)
    return jnp.concatenate([real, moved_on(imag)], axis=0)


def folded(acc):
    real, imag = acc[: CH * CH, :], acc[CH * CH :, :]
    lane = lax.broadcasted_iota(jnp.int32, (CH * CH, HALF), 1)
    right = imag[:, HALF:] + jnp.where(lane == 0, real[:, HALF:], 0.0)
    return jnp.concatenate([real[:, :HALF], right], axis=1)


def kernel(
    n_pairs, n_tm, norm_scale,
    spectra, slot_hbm, tiles_hbm, owners_hbm, table_hbm,
    out,
    slot, tiles, owners, raw, own, from_right, from_left, table,
    diag_acc, low_acc, high_acc,
    diag_out, diag_in, side_out, side_in, hop_out, hop_in, mixed,
    index_sem, raw_sem, table_sem, send_sem, recv_sem, diag_send, diag_recv,
    side_send, side_recv, hop_send, hop_recv,
):
    bins = own.shape[1]
    half_bins = bins // 2
    steps = half_bins // STEP
    here = lax.axis_index("pairs")
    window = lax.axis_index("tm")
    right = (lax.rem(here + 1, n_pairs), window)
    left = (lax.rem(here + n_pairs - 1, n_pairs), window)
    has_right = here < n_pairs - 1
    has_left = here > 0

    def peer(k):
        return lax.rem(window + k, n_tm)

    barrier = pltpu.get_barrier_semaphore()

    def greet(device):
        pl.semaphore_signal(barrier, inc=1, device_id=device, device_id_type=MESH)

    @pl.when(has_right)
    def _():
        greet(right)

    @pl.when(has_left)
    def _():
        greet(left)

    for k in range(1, n_tm):
        greet((here, peer(k)))

    def lanes(index):
        return pl.ds(pl.multiple_of(index * STEP, STEP), STEP)

    order = [part for i in range(steps) for part in (i, steps + i)]

    def raw_copy(part):
        return pltpu.make_async_copy(
            spectra.at[:, :, lanes(part)], raw[part], raw_sem.at[part]
        )

    def table_copy(part):
        return pltpu.make_async_copy(
            table_hbm.at[lanes(part), :], table.at[lanes(part), :], table_sem.at[part]
        )

    index_copies = [
        pltpu.make_async_copy(source, target, index_sem.at[place])
        for place, (source, target) in enumerate(
            [(slot_hbm, slot), (tiles_hbm, tiles), (owners_hbm, owners)]
        )
    ]
    index_copies[0].start()
    for part in order:
        raw_copy(part).start()
    for copy in index_copies[1:]:
        copy.start()
    for part in range(2 * steps):
        table_copy(part).start()

    def low_copy(i):
        return pltpu.make_async_remote_copy(
            own.at[:, lanes(i)], from_right.at[:, lanes(i)],
            send_sem.at[i], recv_sem.at[i], device_id=left, device_id_type=MESH,
        )

    def high_copy(i):
        return pltpu.make_async_remote_copy(
            own.at[:, lanes(steps + i)], from_left.at[:, lanes(i)],
            send_sem.at[steps + i], recv_sem.at[steps + i],
            device_id=right, device_id_type=MESH,
        )

    def send(part):
        if part < steps:

            @pl.when(has_left)
            def _():
                low_copy(part).start()

        else:

            @pl.when(has_right)
            def _():
                high_copy(part - steps).start()

    index_copies[0].wait()
    rows = [slot[c] for c in range(CH)]
    for place, part in enumerate(order):
        raw_copy(part).wait()

        @pl.loop(0, STEP // 1024)
        def _(piece, part=part):
            offset = pl.multiple_of(piece * 1024, 1024)
            values = [raw[part][row, :, pl.ds(offset, 1024)].astype(F32) for row in rows]
            planar = [v[:1] for v in values] + [v[1:] for v in values]
            own[:, pl.ds(pl.multiple_of(part * STEP + offset, 1024), 1024)] = jnp.concatenate(planar, axis=0).astype(BF16)

        if place == steps - 1:
            beside = lax.min(here, 1) + lax.min(n_pairs - 1 - here, 1)
            pl.semaphore_wait(barrier, n_tm - 1 + beside)
            for earlier in order[: place + 1]:
                send(earlier)
        elif place >= steps:
            send(part)

    diag_acc[...] = jnp.zeros_like(diag_acc)
    low_acc[...] = jnp.zeros_like(low_acc)
    high_acc[...] = jnp.zeros_like(high_acc)

    @pl.loop(0, 2 * steps)
    def _(part):
        table_copy(part).wait()
        block = own[:, lanes(part)]
        diag_acc[...] += jnp.dot(
            cross_rows(block, block), table[lanes(part), :], preferred_element_type=F32
        )

    def diag_copy(k):
        return pltpu.make_async_remote_copy(
            diag_out.at[peer(k)], diag_in.at[k], diag_send.at[k], diag_recv.at[k],
            device_id=(here, peer(k)), device_id_type=MESH,
        )

    def side_copy(k):
        return pltpu.make_async_remote_copy(
            side_out.at[peer(k)], side_in.at[k], side_send.at[k], side_recv.at[k],
            device_id=(here, peer(k)), device_id_type=MESH,
        )

    diag = folded(diag_acc[...])
    for t in range(n_tm):
        diag_out[t] = diag[t * CH : (t + 1) * CH]
    for k in range(1, n_tm):
        diag_copy(k).start()

    for copy in index_copies[1:]:
        copy.wait()

    def next_tile(p, carry):
        count, kinds = carry[0], carry[1:]
        mine = owners[p] == here
        kind = 2 * (tiles[0, p] - here + 1) + tiles[1, p] - tiles[0, p]
        kinds = [
            jnp.where(mine & (count == s), kind, kinds[s]) for s in range(TILE_CAP)
        ]
        return (count + mine.astype(jnp.int32), *kinds)

    carry = (jnp.int32(0),) + (jnp.int32(-1),) * TILE_CAP
    kinds = lax.fori_loop(0, tiles.shape[1], next_tile, carry)[1:]

    def low_step(i):
        low_copy(i).wait_recv()
        low_acc[...] += jnp.dot(
            cross_rows(own[:, lanes(i)], from_right[:, lanes(i)]),
            table[lanes(i), :], preferred_element_type=F32,
        )

    def high_step(i):
        high_copy(i).wait_recv()
        high_acc[...] += jnp.dot(
            cross_rows(from_left[:, lanes(i)], own[:, lanes(steps + i)]),
            table[lanes(steps + i), :], preferred_element_type=F32,
        )

    @pl.loop(0, steps)
    def _(i):
        @pl.when(has_right)
        def _():
            low_step(i)

        @pl.when(has_left)
        def _():
            high_step(i)

    low, high = folded(low_acc[...]), folded(high_acc[...])
    for t in range(n_tm):
        side_out[t, :CH] = low[t * CH : (t + 1) * CH]
        side_out[t, CH:] = high[t * CH : (t + 1) * CH]
    for k in range(1, n_tm):
        side_copy(k).start()

    def right_copy(place):
        return pltpu.make_async_remote_copy(
            hop_out.at[place], hop_in.at[place], hop_send.at[place], hop_recv.at[place],
            device_id=right, device_id_type=MESH,
        )

    def left_copy(place):
        return pltpu.make_async_remote_copy(
            hop_out.at[place], hop_in.at[place], hop_send.at[place], hop_recv.at[place],
            device_id=left, device_id_type=MESH,
        )

    diag_sum = diag_out[window]
    for k in range(1, n_tm):
        diag_copy(k).wait_recv()
        diag_sum += diag_in[k]
    hop_out[0] = diag_sum

    @pl.when(has_right)
    def _():
        right_copy(0).start()

    side_sum = side_out[window]
    for k in range(1, n_tm):
        side_copy(k).wait_recv()
        side_sum += side_in[k]
    hop_out[1] = side_sum[:CH]
    hop_out[2] = side_sum[CH:]

    @pl.when(has_right)
    def _():
        right_copy(1).start()

    @pl.when(here > 1)
    def _():
        left_copy(2).start()

    def chosen(s, kind, tile):
        return jnp.where(kinds[s] == kind, tile, 0.0)

    for s in range(TILE_CAP):
        mixed[s] = (
            chosen(s, 1, side_sum[CH:]) + chosen(s, 2, diag_sum) + chosen(s, 3, side_sum[:CH])
        )

    @pl.when(has_left)
    def _():
        right_copy(0).wait_recv()
        right_copy(1).wait_recv()
        for s in range(TILE_CAP):
            mixed[s] += chosen(s, 0, hop_in[0]) + chosen(s, 1, hop_in[1])

    @pl.when(has_left & has_right)
    def _():
        left_copy(2).wait_recv()
        for s in range(TILE_CAP):
            mixed[s] += chosen(s, 3, hop_in[2])

    lane = lax.broadcasted_iota(jnp.int32, (CH, HALF), 1)
    mirror = lax.rem(HALF - lane, HALF)
    for s in range(TILE_CAP):
        even, odd = mixed[s, :, :HALF], mixed[s, :, HALF:]
        before = jnp.where(lane == 0, odd, even - odd)
        before = jnp.take_along_axis(before, mirror, axis=1)
        after = jnp.where(lane == 0, even, even + odd)
        out[s] = jnp.concatenate([before, after], axis=1) * norm_scale

    @pl.when(has_left)
    def _():
        for i in range(steps):
            low_copy(i).wait_send()

    @pl.when(has_right)
    def _():
        for i in range(steps):
            high_copy(i).wait_send()
        right_copy(0).wait_send()
        right_copy(1).wait_send()

    @pl.when(here > 1)
    def _():
        left_copy(2).wait_send()

    for k in range(1, n_tm):
        diag_copy(k).wait_send()
        side_copy(k).wait_send()


def on_device(n_pairs, n_tm, spectra, channel_slot, tile_list, tile_owner):
    bins = spectra.shape[3]
    steps = bins // 2 // STEP
    dma = pltpu.SemaphoreType.DMA
    vmem = pl.BlockSpec(memory_space=pltpu.VMEM)
    hbm = pl.BlockSpec(memory_space=pl.ANY)
    return pl.pallas_call(
        functools.partial(kernel, n_pairs, n_tm, 1.0 / math.sqrt(2.0 * bins * n_tm)),
        out_shape=jax.ShapeDtypeStruct((TILE_CAP, CH, LAGS), F32),
        in_specs=[hbm] * 5,
        out_specs=vmem,
        scratch_shapes=[
            pltpu.SMEM(channel_slot.shape, jnp.int32),
            pltpu.SMEM(tile_list.shape[::-1], jnp.int32),
            pltpu.SMEM(tile_owner.shape, jnp.int32),
            [pltpu.VMEM((CH, 2, STEP), BF16) for _ in range(2 * steps)],
            pltpu.VMEM((2 * CH, bins), BF16),
            pltpu.VMEM((2 * CH, bins // 2), BF16),
            pltpu.VMEM((2 * CH, bins // 2), BF16),
            pltpu.VMEM((bins, LAGS), BF16),
            pltpu.VMEM((2 * CH * CH, LAGS), F32),
            pltpu.VMEM((2 * CH * CH, LAGS), F32),
            pltpu.VMEM((2 * CH * CH, LAGS), F32),
            pltpu.VMEM((n_tm, CH, LAGS), F32),
            pltpu.VMEM((n_tm, CH, LAGS), F32),
            pltpu.VMEM((n_tm, 2 * CH, LAGS), F32),
            pltpu.VMEM((n_tm, 2 * CH, LAGS), F32),
            pltpu.VMEM((3, CH, LAGS), F32),
            pltpu.VMEM((3, CH, LAGS), F32),
            pltpu.VMEM((TILE_CAP, CH, LAGS), F32),
            dma((3,)),
            dma((2 * steps,)),
            dma((2 * steps,)),
            dma((2 * steps,)),
            dma((2 * steps,)),
            dma((n_tm,)),
            dma((n_tm,)),
            dma((n_tm,)),
            dma((n_tm,)),
            dma((3,)),
            dma((3,)),
        ],
        compiler_params=pltpu.CompilerParams(
            collective_id=0, has_side_effects=True, vmem_limit_bytes=63 * 1024 * 1024
        ),
    )(spectra[0], channel_slot, tile_list.T, tile_owner, jnp.asarray(lag_table(bins)))


def solution(mesh):
    placed = (P("tm", "pairs", None, None), P("pairs"), P(), P())
    body = functools.partial(on_device, mesh.shape["pairs"], mesh.shape["tm"])
    return jax.shard_map(
        body, mesh=mesh, in_specs=placed, out_specs=P("pairs", "tm", None), check_vma=False
    )
```

```python
import functools
import math

import jax
import jax.numpy as jnp
import ml_dtypes
import numpy as np
from jax import lax
from jax.experimental import pallas as pl
from jax.experimental.pallas import tpu as pltpu
from jax.sharding import PartitionSpec as P

LAGS = 256
TILE_CAP = 4
CH = 8
HALF = LAGS // 2
TURN = 512
SHIFT = TURN // 4
STEP = 4096
MESH = pl.DeviceIdType.MESH
F32 = jnp.float32
BF16 = jnp.bfloat16


def lag_table(bins):
    bin_ids = np.arange(bins)
    turn_start = bin_ids // TURN * TURN
    moved = turn_start + (bin_ids - turn_start + SHIFT) % TURN

    def phase(ids, lags):
        steps = (ids[:, None] * lags[None, :]) % (2 * bins)
        return (steps.astype(np.float32) * np.float32(math.pi / bins)).astype(np.float64)

    cosine = np.cos(phase(bin_ids, np.arange(HALF)))
    sine = -np.sin(phase(moved, np.arange(HALF)))
    sine[:, :1] = np.cos(phase(bin_ids, np.array([HALF])))
    joined = np.concatenate([cosine, sine], axis=1)
    return joined.astype(np.float32).astype(ml_dtypes.bfloat16)


def moved_on(block):
    parts = []
    for start in range(0, block.shape[1], TURN):
        parts.append(block[:, start + SHIFT : start + TURN])
        parts.append(block[:, start : start + SHIFT])
    return jnp.concatenate(parts, axis=1)


def cross_rows(lead, tail):
    lead = lead.astype(F32)
    tail = tail.astype(F32)
    tail_re, tail_im = tail[:CH], tail[CH:]
    real, imag = [], []
    for a in range(CH):
        lead_re, lead_im = lead[a : a + 1], lead[CH + a : CH + a + 1]
        real.append(lead_re * tail_re + lead_im * tail_im)
        imag.append(lead_im * tail_re - lead_re * tail_im)
    real = jnp.concatenate(real, axis=0).astype(BF16)
    imag = jnp.concatenate(imag, axis=0).astype(BF16)
    return jnp.concatenate([real, moved_on(imag)], axis=0)


def folded(acc):
    real, imag = acc[: CH * CH, :], acc[CH * CH :, :]
    lane = lax.broadcasted_iota(jnp.int32, (CH * CH, HALF), 1)
    right = imag[:, HALF:] + jnp.where(lane == 0, real[:, HALF:], 0.0)
    return jnp.concatenate([real[:, :HALF], right], axis=1)


def kernel(
    n_pairs, n_tm, norm_scale,
    spectra, slot_hbm, tiles_hbm, owners_hbm, table_hbm,
    out,
    slot, tiles, owners, raw, own, beside, table,
    diag_acc, side_acc, diag_out, diag_in, hop_out, hop_in,
    side_out, arrived, mixed,
    index_sem, raw_sem, table_sem, send_sem, recv_sem, diag_send, diag_recv,
    hop_send, hop_recv, own_send, near_send, arrived_sem,
):
    bins = own.shape[1]
    steps = bins // STEP
    here = lax.axis_index("pairs")
    window = lax.axis_index("tm")
    odd = lax.rem(window, 2)
    even_window = odd == 0
    right = lax.rem(here + 1, n_pairs)
    left = lax.rem(here + n_pairs - 1, n_pairs)
    near = lax.rem(here + 1 - 2 * odd + n_pairs, n_pairs)
    away = lax.rem(here - 1 + 2 * odd + n_pairs, n_pairs)
    to_right = lax.min(n_pairs - 1 - here, 1)
    to_left = lax.min(here, 1)
    has_right = to_right == 1
    has_left = to_left == 1
    to_near = to_right * (1 - odd) + to_left * odd
    to_away = to_left * (1 - odd) + to_right * odd
    has_near = to_near == 1
    has_away = to_away == 1
    gives_own = has_left
    gives_near = has_near & (here * odd != 1)

    def peer(k):
        return lax.rem(window + k, n_tm)

    barrier = pltpu.get_barrier_semaphore()

    def greet(block, t):
        pl.semaphore_signal(barrier, inc=1, device_id=(block, t), device_id_type=MESH)

    @pl.when(has_right)
    def _():
        for t in range(1, n_tm, 2):
            greet(right, t)

        @pl.when(even_window)
        def _():
            greet(right, window)

    @pl.when(has_left)
    def _():
        for t in range(0, n_tm, 2):
            greet(left, t)

        @pl.when(odd == 1)
        def _():
            greet(left, window)

    for k in range(1, n_tm):
        greet(here, peer(k))

    def lanes(index):
        return pl.ds(pl.multiple_of(index * STEP, STEP), STEP)

    def raw_copy(part):
        return pltpu.make_async_copy(
            spectra.at[:, :, lanes(part)], raw[part], raw_sem.at[part]
        )

    def table_copy(part):
        return pltpu.make_async_copy(
            table_hbm.at[lanes(part), :], table.at[lanes(part), :], table_sem.at[part]
        )

    index_copies = [
        pltpu.make_async_copy(source, target, index_sem.at[place])
        for place, (source, target) in enumerate(
            [(slot_hbm, slot), (tiles_hbm, tiles), (owners_hbm, owners)]
        )
    ]
    index_copies[0].start()
    for part in range(steps):
        raw_copy(part).start()
    for copy in index_copies[1:]:
        copy.start()
    def block_copy(span, place):
        return pltpu.make_async_remote_copy(
            own.at[:, span], beside.at[:, span], send_sem.at[0], recv_sem.at[place],
            device_id=(away, window), device_id_type=MESH,
        )

    last = [
        (pl.ds((steps - 1) * STEP + i * STEP // 2, STEP // 2), steps - 1 + i) for i in range(2)
    ]

    index_copies[0].wait()
    rows = [slot[c] for c in range(CH)]
    entered = 1
    for part in range(steps):
        raw_copy(part).wait()

        @pl.loop(0, STEP // 1024)
        def _(piece, part=part):
            offset = pl.multiple_of(piece * 1024, 1024)
            values = [raw[part][row, :, pl.ds(offset, 1024)].astype(F32) for row in rows]
            planar = [v[:1] for v in values] + [v[1:] for v in values]
            own[:, pl.ds(pl.multiple_of(part * STEP + offset, 1024), 1024)] = jnp.concatenate(
                planar, axis=0
            ).astype(BF16)

        if part == entered:
            pl.semaphore_wait(barrier, n_tm - 1 + n_tm * to_near + to_away)
        if part >= entered:

            @pl.when(has_away)
            def _(part=part):
                for ready in range(0 if part == entered else part, part + 1):
                    pieces = last if ready == steps - 1 else [(lanes(ready), ready)]
                    for span, place in pieces:
                        block_copy(span, place).start()

    for part in range(steps):
        table_copy(part).start()

    diag_acc[...] = jnp.zeros_like(diag_acc)
    side_acc[...] = jnp.zeros_like(side_acc)

    @pl.loop(0, steps)
    def _(part):
        table_copy(part).wait()
        block = own[:, lanes(part)]
        diag_acc[...] += jnp.dot(
            cross_rows(block, block), table[lanes(part), :], preferred_element_type=F32
        )

    def diag_copy(k):
        return pltpu.make_async_remote_copy(
            diag_out.at[peer(k)], diag_in.at[k - 1], diag_send.at[0], diag_recv.at[0],
            device_id=(here, peer(k)), device_id_type=MESH,
        )

    diag_all = pltpu.make_async_remote_copy(
        diag_out.at[pl.ds(0, n_tm - 1)], diag_in, diag_send.at[0], diag_recv.at[0],
        device_id=(here, peer(1)), device_id_type=MESH,
    )
    far_first = sorted(range(1, n_tm), key=lambda k: abs(k - n_tm // 2))

    diag = folded(diag_acc[...])
    for t in range(n_tm):
        diag_out[t] = diag[t * CH : (t + 1) * CH]
    for k in far_first:
        diag_copy(k).start()

    for copy in index_copies[1:]:
        copy.wait()

    def next_tile(p, carry):
        count, kinds = carry[0], carry[1:]
        mine = owners[p] == here
        kind = 2 * (tiles[0, p] - here + 1) + tiles[1, p] - tiles[0, p]
        kinds = [
            jnp.where(mine & (count == s), kind, kinds[s]) for s in range(TILE_CAP)
        ]
        return (count + mine.astype(jnp.int32), *kinds)

    carry = (jnp.int32(0),) + (jnp.int32(-1),) * TILE_CAP
    kinds = lax.fori_loop(0, tiles.shape[1], next_tile, carry)[1:]

    def chosen(s, kind, tile):
        return jnp.where(kinds[s] == kind, tile, 0.0)

    def side_step(span, place):
        block_copy(span, place).wait_recv()
        mine = own[:, span].astype(F32)
        other = beside[:, span].astype(F32)
        lead = jnp.where(even_window, mine, other)
        tail = jnp.where(even_window, other, mine)
        side_acc[...] += jnp.dot(
            cross_rows(lead, tail), table[span, :], preferred_element_type=F32
        )

    hop = pltpu.make_async_remote_copy(
        hop_out, hop_in, hop_send.at[0], hop_recv.at[0],
        device_id=(right, window), device_id_type=MESH,
    )

    @pl.loop(0, steps - 2)
    def _(part):
        @pl.when(has_near)
        def _():
            side_step(lanes(part), part)

    diag_all.wait_recv()
    diag_sum = diag_out[window]
    for k in range(n_tm - 1):
        diag_sum += diag_in[k]
    hop_out[...] = diag_sum

    @pl.when(has_right)
    def _():
        hop.start()

    @pl.when(has_near)
    def _():
        side_step(lanes(steps - 2), steps - 2)
        for span, place in last:
            side_step(span, place)

    def own_copy(k):
        return pltpu.make_async_remote_copy(
            side_out.at[peer(k)], arrived.at[window], own_send.at[0], arrived_sem.at[0],
            device_id=(here, peer(k)), device_id_type=MESH,
        )

    def right_copy(k):
        return pltpu.make_async_remote_copy(
            side_out.at[peer(k)], arrived.at[n_tm + window // 2],
            near_send.at[0], arrived_sem.at[0],
            device_id=(right, peer(k)), device_id_type=MESH,
        )

    def left_copy(k):
        return pltpu.make_async_remote_copy(
            side_out.at[peer(k)], arrived.at[n_tm + n_tm // 2 + window // 2],
            near_send.at[0], arrived_sem.at[0],
            device_id=(left, peer(k)), device_id_type=MESH,
        )

    def several(buffer, count, send):
        return pltpu.make_async_remote_copy(
            buffer.at[pl.ds(0, count)], buffer.at[pl.ds(0, count)], send, arrived_sem.at[0],
            device_id=(right, window), device_id_type=MESH,
        )

    side = folded(side_acc[...])
    for t in range(n_tm):
        side_out[t] = side[t * CH : (t + 1) * CH]

    @pl.when(gives_near)
    def _():
        @pl.when(even_window)
        def _():
            for k in far_first + [0]:
                right_copy(k).start()

        @pl.when(odd == 1)
        def _():
            for k in far_first + [0]:
                left_copy(k).start()

    @pl.when(gives_own)
    def _():
        for k in far_first:
            own_copy(k).start()

    arrived[window] = side_out[window]
    for s in range(TILE_CAP):
        mixed[s] = chosen(s, 2, diag_sum)

    @pl.when(has_away)
    def _():
        pltpu.make_async_remote_copy(
            own, beside, send_sem.at[0], recv_sem.at[0],
            device_id=(away, window), device_id_type=MESH,
        ).wait_send()

    diag_all.wait_send()

    @pl.when(has_right)
    def _():
        hop.wait_send()

    @pl.when(has_left)
    def _():
        hop.wait_recv()
        for s in range(TILE_CAP):
            mixed[s] += chosen(s, 0, hop_in[...])

    @pl.when(has_left & has_right)
    def _():
        several(arrived, 2 * n_tm - 1, own_send.at[0]).wait_recv()
        after = arrived[0]
        for place in range(2, n_tm, 2):
            after += arrived[place]
        for place in range(n_tm + n_tm // 2, 2 * n_tm):
            after += arrived[place]
        for s in range(TILE_CAP):
            mixed[s] += chosen(s, 3, after)

    @pl.when(has_left & (to_right == 0))
    def _():
        several(arrived, n_tm - 1 + n_tm // 2, own_send.at[0]).wait_recv()

    @pl.when(has_left)
    def _():
        before = arrived[1]
        for place in range(3, n_tm, 2):
            before += arrived[place]
        for place in range(n_tm, n_tm + n_tm // 2):
            before += arrived[place]
        for s in range(TILE_CAP):
            mixed[s] += chosen(s, 1, before)

    lane = lax.broadcasted_iota(jnp.int32, (CH, HALF), 1)
    mirror = lax.rem(HALF - lane, HALF)
    for s in range(TILE_CAP):
        cosine, sine = mixed[s, :, :HALF], mixed[s, :, HALF:]
        before = jnp.where(lane == 0, sine, cosine - sine)
        before = jnp.take_along_axis(before, mirror, axis=1)
        after = jnp.where(lane == 0, cosine, cosine + sine)
        out[s] = jnp.concatenate([before, after], axis=1) * norm_scale

    @pl.when(gives_near)
    def _():
        several(arrived, n_tm, near_send.at[0]).wait_send()

    @pl.when(gives_own)
    def _():
        several(arrived, n_tm - 1, own_send.at[0]).wait_send()


def on_device(n_pairs, n_tm, spectra, channel_slot, tile_list, tile_owner):
    bins = spectra.shape[3]
    steps = bins // STEP
    dma = pltpu.SemaphoreType.DMA
    vmem = pl.BlockSpec(memory_space=pltpu.VMEM)
    hbm = pl.BlockSpec(memory_space=pl.ANY)
    group = pltpu.VMEM((n_tm, CH, LAGS), F32)
    share = pltpu.VMEM((CH, LAGS), F32)
    return pl.pallas_call(
        functools.partial(kernel, n_pairs, n_tm, 1.0 / math.sqrt(2.0 * bins * n_tm)),
        out_shape=jax.ShapeDtypeStruct((TILE_CAP, CH, LAGS), F32),
        in_specs=[hbm] * 5,
        out_specs=vmem,
        scratch_shapes=[
            pltpu.SMEM(channel_slot.shape, jnp.int32),
            pltpu.SMEM(tile_list.shape[::-1], jnp.int32),
            pltpu.SMEM(tile_owner.shape, jnp.int32),
            [pltpu.VMEM((CH, 2, STEP), BF16) for _ in range(steps)],
            pltpu.VMEM((2 * CH, bins), BF16),
            pltpu.VMEM((2 * CH, bins), BF16),
            pltpu.VMEM((bins, LAGS), BF16),
            pltpu.VMEM((2 * CH * CH, LAGS), F32),
            pltpu.VMEM((2 * CH * CH, LAGS), F32),
            group,
            pltpu.VMEM((n_tm - 1, CH, LAGS), F32),
            share,
            share,
            group,
            pltpu.VMEM((2 * n_tm, CH, LAGS), F32),
            pltpu.VMEM((TILE_CAP, CH, LAGS), F32),
            dma((3,)),
            dma((steps,)),
            dma((steps,)),
            dma((1,)),
            dma((steps + 1,)),
            dma((1,)),
            dma((1,)),
            dma((1,)),
            dma((1,)),
            dma((1,)),
            dma((1,)),
            dma((1,)),
        ],
        compiler_params=pltpu.CompilerParams(
            collective_id=0, has_side_effects=True, vmem_limit_bytes=63 * 1024 * 1024
        ),
    )(spectra[0], channel_slot, tile_list.T, tile_owner, jnp.asarray(lag_table(bins)))


def solution(mesh):
    placed = (P("tm", "pairs", None, None), P("pairs"), P(), P())
    body = functools.partial(on_device, mesh.shape["pairs"], mesh.shape["tm"])
    return jax.shard_map(
        body, mesh=mesh, in_specs=placed, out_specs=P("pairs", "tm", None), check_vma=False
    )
```

```python
import functools
import math

import jax
import jax.numpy as jnp
import ml_dtypes
import numpy as np
from jax import lax
from jax.experimental import pallas as pl
from jax.experimental.pallas import tpu as pltpu
from jax.sharding import PartitionSpec as P

LAGS = 256
TILE_CAP = 4
CH = 8
HALF = LAGS // 2
TURN = 512
SHIFT = TURN // 4
STEP = 4096
PIECE = STEP // 2
ROW = 8
MOVED = 2 * PIECE
MESH = pl.DeviceIdType.MESH
F32 = jnp.float32
BF16 = jnp.bfloat16


def lag_table(bins):
    bin_ids = np.arange(bins)
    turn_start = bin_ids // TURN * TURN
    moved = turn_start + (bin_ids - turn_start + SHIFT) % TURN

    def phase(ids, lags):
        steps = (ids[:, None] * lags[None, :]) % (2 * bins)
        return (steps.astype(np.float32) * np.float32(math.pi / bins)).astype(np.float64)

    cosine = np.cos(phase(bin_ids, np.arange(HALF)))
    sine = -np.sin(phase(moved, np.arange(HALF)))
    sine[:, :1] = np.cos(phase(bin_ids, np.array([HALF])))
    joined = np.concatenate([cosine, sine], axis=1)
    return joined.astype(np.float32).astype(ml_dtypes.bfloat16)


def moved_on(block):
    parts = []
    for start in range(0, block.shape[1], TURN):
        parts.append(block[:, start + SHIFT : start + TURN])
        parts.append(block[:, start : start + SHIFT])
    return jnp.concatenate(parts, axis=1)


def cross_rows(lead, tail):
    lead = lead.astype(F32)
    tail = tail.astype(F32)
    tail_re, tail_im = tail[:CH], tail[CH:]
    real, imag = [], []
    for a in range(CH):
        lead_re, lead_im = lead[a : a + 1], lead[CH + a : CH + a + 1]
        real.append(lead_re * tail_re + lead_im * tail_im)
        imag.append(lead_im * tail_re - lead_re * tail_im)
    real = jnp.concatenate(real, axis=0).astype(BF16)
    imag = jnp.concatenate(imag, axis=0).astype(BF16)
    return jnp.concatenate([real, moved_on(imag)], axis=0)


def folded(acc):
    real, imag = acc[: CH * CH, :], acc[CH * CH :, :]
    lane = lax.broadcasted_iota(jnp.int32, (CH * CH, HALF), 1)
    right = imag[:, HALF:] + jnp.where(lane == 0, real[:, HALF:], 0.0)
    return jnp.concatenate([real[:, :HALF], right], axis=1)


def kernel(
    n_pairs, n_tm, norm_scale,
    spectra, slot_hbm, tiles_hbm, owners_hbm, table_hbm,
    out,
    slot, tiles, owners, raw, own, beside, table,
    diag_acc, side_acc, diag_out, diag_in, hop_out, hop_in,
    side_out, arrived, mixed, moved_lead, moved_tail,
    index_sem, raw_sem, table_sem, send_sem, recv_sem, diag_send, diag_recv,
    hop_send, hop_recv, own_send, near_send, arrived_sem, moved_send, moved_recv,
):
    bins = own.shape[1]
    steps = bins // STEP
    here = lax.axis_index("pairs")
    window = lax.axis_index("tm")
    odd = lax.rem(window, 2)
    even_window = odd == 0
    right = lax.rem(here + 1, n_pairs)
    left = lax.rem(here + n_pairs - 1, n_pairs)
    near = lax.rem(here + 1 - 2 * odd + n_pairs, n_pairs)
    away = lax.rem(here - 1 + 2 * odd + n_pairs, n_pairs)
    to_right = lax.min(n_pairs - 1 - here, 1)
    to_left = lax.min(here, 1)
    has_right = to_right == 1
    has_left = to_left == 1
    to_near = to_right * (1 - odd) + to_left * odd
    to_away = to_left * (1 - odd) + to_right * odd
    has_near = to_near == 1
    has_away = to_away == 1
    gives_own = has_left
    starts_row = to_left * (1 - lax.min(lax.rem(here, ROW), 1))
    ends_row = to_right * (1 - lax.min(ROW - 1 - lax.rem(here, ROW), 1))
    gives_tail = starts_row * (1 - odd) == 1
    gives_lead = ends_row * (1 - odd) == 1
    takes_moved = starts_row * odd == 1
    gives_near = has_near & (here * odd != 1)

    def peer(k):
        return lax.rem(window + k, n_tm)

    barrier = pltpu.get_barrier_semaphore()

    def greet(block, t):
        pl.semaphore_signal(barrier, inc=1, device_id=(block, t), device_id_type=MESH)

    @pl.when(has_right)
    def _():
        greet(right, window)

    @pl.when(has_left)
    def _():
        greet(left, window)

    @pl.when(takes_moved)
    def _():
        greet(left, window - 1)

    far_first = sorted(range(1, n_tm), key=lambda k: abs(k - n_tm // 2))
    for k in far_first:
        greet(here, peer(k))

    def lanes(index):
        return pl.ds(pl.multiple_of(index * STEP, STEP), STEP)

    def raw_copy(part):
        return pltpu.make_async_copy(
            spectra.at[:, :, lanes(part)], raw[part], raw_sem.at[part]
        )

    def table_copy(part):
        return pltpu.make_async_copy(
            table_hbm.at[lanes(part), :], table.at[lanes(part), :], table_sem.at[part]
        )

    index_copies = [
        pltpu.make_async_copy(source, target, index_sem.at[place])
        for place, (source, target) in enumerate(
            [(slot_hbm, slot), (tiles_hbm, tiles), (owners_hbm, owners)]
        )
    ]
    index_copies[0].start()
    for part in range(steps):
        raw_copy(part).start()
    for copy in index_copies[1:]:
        copy.start()
    def block_copy(span, place):
        return pltpu.make_async_remote_copy(
            own.at[:, span], beside.at[:, span], send_sem.at[0], recv_sem.at[place],
            device_id=(away, window), device_id_type=MESH,
        )

    kept = bins - MOVED
    pieces = [
        (pl.ds(start, PIECE), steps - 2 + i)
        for i, start in enumerate(range(bins - 2 * STEP, bins, PIECE))
    ]
    moved_span = pl.ds(kept, MOVED)
    tail_copy = pltpu.make_async_remote_copy(
        own.at[:, moved_span], moved_tail, moved_send.at[0], moved_recv.at[0],
        device_id=(here, lax.rem(window + 1, n_tm)), device_id_type=MESH,
    )
    lead_copy = pltpu.make_async_remote_copy(
        own.at[:, moved_span], moved_lead, moved_send.at[0], moved_recv.at[1],
        device_id=(right, lax.rem(window + 1, n_tm)), device_id_type=MESH,
    )

    index_copies[0].wait()
    rows = [slot[c] for c in range(CH)]
    entered = 1
    for part in range(steps):
        raw_copy(part).wait()

        @pl.loop(0, STEP // 1024)
        def _(piece, part=part):
            offset = pl.multiple_of(piece * 1024, 1024)
            values = [raw[part][row, :, pl.ds(offset, 1024)].astype(F32) for row in rows]
            planar = [v[:1] for v in values] + [v[1:] for v in values]
            own[:, pl.ds(pl.multiple_of(part * STEP + offset, 1024), 1024)] = jnp.concatenate(
                planar, axis=0
            ).astype(BF16)

        if part == entered:
            pl.semaphore_wait(
                barrier, n_tm - 1 + to_left + to_right + ends_row * (1 - odd)
            )
        if entered <= part < steps - 2:

            @pl.when(has_away)
            def _(part=part):
                for ready in range(0 if part == entered else part, part + 1):
                    block_copy(lanes(ready), ready).start()

        if part >= steps - 2:
            for span, place in pieces[2 * (part - steps + 2) :][:2]:
                needed = has_away if span.start < kept else has_away & ~gives_tail

                @pl.when(needed)
                def _(span=span, place=place):
                    block_copy(span, place).start()

    @pl.when(gives_tail)
    def _():
        tail_copy.start()

    @pl.when(gives_lead)
    def _():
        lead_copy.start()

    for part in range(steps):
        table_copy(part).start()

    diag_acc[...] = jnp.zeros_like(diag_acc)
    side_acc[...] = jnp.zeros_like(side_acc)

    @pl.loop(0, steps)
    def _(part):
        table_copy(part).wait()
        block = own[:, lanes(part)]
        diag_acc[...] += jnp.dot(
            cross_rows(block, block), table[lanes(part), :], preferred_element_type=F32
        )

    def diag_copy(k):
        return pltpu.make_async_remote_copy(
            diag_out.at[peer(k)], diag_in.at[k - 1], diag_send.at[0], diag_recv.at[0],
            device_id=(here, peer(k)), device_id_type=MESH,
        )

    diag_all = pltpu.make_async_remote_copy(
        diag_out.at[pl.ds(0, n_tm - 1)], diag_in, diag_send.at[0], diag_recv.at[0],
        device_id=(here, peer(1)), device_id_type=MESH,
    )
    diag = folded(diag_acc[...])
    for t in range(n_tm):
        diag_out[t] = diag[t * CH : (t + 1) * CH]
    for k in far_first:
        diag_copy(k).start()

    for copy in index_copies[1:]:
        copy.wait()

    def next_tile(p, carry):
        count, kinds = carry[0], carry[1:]
        mine = owners[p] == here
        kind = 2 * (tiles[0, p] - here + 1) + tiles[1, p] - tiles[0, p]
        kinds = [
            jnp.where(mine & (count == s), kind, kinds[s]) for s in range(TILE_CAP)
        ]
        return (count + mine.astype(jnp.int32), *kinds)

    carry = (jnp.int32(0),) + (jnp.int32(-1),) * TILE_CAP
    kinds = lax.fori_loop(0, tiles.shape[1], next_tile, carry)[1:]

    def chosen(s, kind, tile):
        return jnp.where(kinds[s] == kind, tile, 0.0)

    def side_sum(lead, tail, span):
        side_acc[...] += jnp.dot(
            cross_rows(lead, tail), table[span, :], preferred_element_type=F32
        )

    def side_step(span, place):
        block_copy(span, place).wait_recv()
        mine = own[:, span].astype(F32)
        other = beside[:, span].astype(F32)
        side_sum(
            jnp.where(even_window, mine, other), jnp.where(even_window, other, mine), span
        )

    hop = pltpu.make_async_remote_copy(
        hop_out, hop_in, hop_send.at[0], hop_recv.at[0],
        device_id=(right, window), device_id_type=MESH,
    )

    @pl.loop(0, steps - 2)
    def _(part):
        @pl.when(has_near)
        def _():
            side_step(lanes(part), part)

    diag_all.wait_recv()
    diag_sum = diag_out[window]
    for k in range(n_tm - 1):
        diag_sum += diag_in[k]
    hop_out[...] = diag_sum

    @pl.when(has_right)
    def _():
        hop.start()

    @pl.when(takes_moved)
    def _():
        tail_copy.wait_recv()
        lead_copy.wait_recv()
        for start in range(0, MOVED, PIECE):
            part = pl.ds(start, PIECE)
            side_sum(moved_lead[:, part], moved_tail[:, part], pl.ds(kept + start, PIECE))

    for span, place in pieces:
        needed = has_near if span.start < kept else has_near & ~gives_lead

        @pl.when(needed)
        def _(span=span, place=place):
            side_step(span, place)

    def own_copy(k):
        return pltpu.make_async_remote_copy(
            side_out.at[peer(k)], arrived.at[window], own_send.at[0], arrived_sem.at[0],
            device_id=(here, peer(k)), device_id_type=MESH,
        )

    def right_copy(k):
        return pltpu.make_async_remote_copy(
            side_out.at[peer(k)], arrived.at[n_tm + window // 2],
            near_send.at[0], arrived_sem.at[0],
            device_id=(right, peer(k)), device_id_type=MESH,
        )

    def left_copy(k):
        return pltpu.make_async_remote_copy(
            side_out.at[peer(k)], arrived.at[n_tm + n_tm // 2 + window // 2],
            near_send.at[0], arrived_sem.at[0],
            device_id=(left, peer(k)), device_id_type=MESH,
        )

    def several(buffer, count, send):
        return pltpu.make_async_remote_copy(
            buffer.at[pl.ds(0, count)], buffer.at[pl.ds(0, count)], send, arrived_sem.at[0],
            device_id=(right, window), device_id_type=MESH,
        )

    side = folded(side_acc[...])
    for t in range(n_tm):
        side_out[t] = side[t * CH : (t + 1) * CH]

    @pl.when(gives_near)
    def _():
        @pl.when(even_window)
        def _():
            for k in far_first + [0]:
                right_copy(k).start()

        @pl.when(odd == 1)
        def _():
            for k in far_first + [0]:
                left_copy(k).start()

    @pl.when(gives_own)
    def _():
        for k in far_first:
            own_copy(k).start()

    arrived[window] = side_out[window]
    for s in range(TILE_CAP):
        mixed[s] = chosen(s, 2, diag_sum)

    def sent(span):
        pltpu.make_async_remote_copy(
            own.at[:, span], beside.at[:, span], send_sem.at[0], recv_sem.at[0],
            device_id=(away, window), device_id_type=MESH,
        ).wait_send()

    @pl.when(has_away & ~gives_tail)
    def _():
        sent(pl.ds(0, bins))

    @pl.when(gives_tail)
    def _():
        sent(pl.ds(0, kept))
        tail_copy.wait_send()

    @pl.when(gives_lead)
    def _():
        lead_copy.wait_send()

    diag_all.wait_send()

    @pl.when(has_right)
    def _():
        hop.wait_send()

    @pl.when(has_left)
    def _():
        hop.wait_recv()
        for s in range(TILE_CAP):
            mixed[s] += chosen(s, 0, hop_in[...])

    @pl.when(has_left & has_right)
    def _():
        several(arrived, 2 * n_tm - 1, own_send.at[0]).wait_recv()
        after = arrived[0]
        for place in range(2, n_tm, 2):
            after += arrived[place]
        for place in range(n_tm + n_tm // 2, 2 * n_tm):
            after += arrived[place]
        for s in range(TILE_CAP):
            mixed[s] += chosen(s, 3, after)

    @pl.when(has_left & (to_right == 0))
    def _():
        several(arrived, n_tm - 1 + n_tm // 2, own_send.at[0]).wait_recv()

    @pl.when(has_left)
    def _():
        before = arrived[1]
        for place in range(3, n_tm, 2):
            before += arrived[place]
        for place in range(n_tm, n_tm + n_tm // 2):
            before += arrived[place]
        for s in range(TILE_CAP):
            mixed[s] += chosen(s, 1, before)

    lane = lax.broadcasted_iota(jnp.int32, (CH, HALF), 1)
    mirror = lax.rem(HALF - lane, HALF)
    for s in range(TILE_CAP):
        cosine, sine = mixed[s, :, :HALF], mixed[s, :, HALF:]
        before = jnp.where(lane == 0, sine, cosine - sine)
        before = jnp.take_along_axis(before, mirror, axis=1)
        after = jnp.where(lane == 0, cosine, cosine + sine)
        out[s] = jnp.concatenate([before, after], axis=1) * norm_scale

    @pl.when(gives_near)
    def _():
        several(arrived, n_tm, near_send.at[0]).wait_send()

    @pl.when(gives_own)
    def _():
        several(arrived, n_tm - 1, own_send.at[0]).wait_send()


def on_device(n_pairs, n_tm, spectra, channel_slot, tile_list, tile_owner):
    bins = spectra.shape[3]
    steps = bins // STEP
    dma = pltpu.SemaphoreType.DMA
    vmem = pl.BlockSpec(memory_space=pltpu.VMEM)
    hbm = pl.BlockSpec(memory_space=pl.ANY)
    group = pltpu.VMEM((n_tm, CH, LAGS), F32)
    share = pltpu.VMEM((CH, LAGS), F32)
    return pl.pallas_call(
        functools.partial(kernel, n_pairs, n_tm, 1.0 / math.sqrt(2.0 * bins * n_tm)),
        out_shape=jax.ShapeDtypeStruct((TILE_CAP, CH, LAGS), F32),
        in_specs=[hbm] * 5,
        out_specs=vmem,
        scratch_shapes=[
            pltpu.SMEM(channel_slot.shape, jnp.int32),
            pltpu.SMEM(tile_list.shape[::-1], jnp.int32),
            pltpu.SMEM(tile_owner.shape, jnp.int32),
            [pltpu.VMEM((CH, 2, STEP), BF16) for _ in range(steps)],
            pltpu.VMEM((2 * CH, bins), BF16),
            pltpu.VMEM((2 * CH, bins), BF16),
            pltpu.VMEM((bins, LAGS), BF16),
            pltpu.VMEM((2 * CH * CH, LAGS), F32),
            pltpu.VMEM((2 * CH * CH, LAGS), F32),
            group,
            pltpu.VMEM((n_tm - 1, CH, LAGS), F32),
            share,
            share,
            group,
            pltpu.VMEM((2 * n_tm, CH, LAGS), F32),
            pltpu.VMEM((TILE_CAP, CH, LAGS), F32),
            pltpu.VMEM((2 * CH, MOVED), BF16),
            pltpu.VMEM((2 * CH, MOVED), BF16),
            dma((3,)),
            dma((steps,)),
            dma((steps,)),
            dma((1,)),
            dma((steps + 2,)),
            dma((1,)),
            dma((1,)),
            dma((1,)),
            dma((1,)),
            dma((1,)),
            dma((1,)),
            dma((1,)),
            dma((1,)),
            dma((2,)),
        ],
        compiler_params=pltpu.CompilerParams(
            collective_id=0, has_side_effects=True, vmem_limit_bytes=63 * 1024 * 1024
        ),
    )(spectra[0], channel_slot, tile_list.T, tile_owner, jnp.asarray(lag_table(bins)))


def solution(mesh):
    placed = (P("tm", "pairs", None, None), P("pairs"), P(), P())
    body = functools.partial(on_device, mesh.shape["pairs"], mesh.shape["tm"])
    return jax.shard_map(
        body, mesh=mesh, in_specs=placed, out_specs=P("pairs", "tm", None), check_vma=False
    )
```

```python
import functools
import math

import jax
import jax.numpy as jnp
import ml_dtypes
import numpy as np
from jax import lax
from jax.experimental import pallas as pl
from jax.experimental.pallas import tpu as pltpu
from jax.sharding import PartitionSpec as P

LAGS = 256
TILE_CAP = 4
CH = 8
HALF = LAGS // 2
TURN = 512
SHIFT = TURN // 4
STEP = 4096
PIECE = STEP // 2
ROW = 8
MOVED = 2 * PIECE
MESH = pl.DeviceIdType.MESH
F32 = jnp.float32
BF16 = jnp.bfloat16


def lag_table(bins):
    bin_ids = np.arange(bins)
    turn_start = bin_ids // TURN * TURN
    moved = turn_start + (bin_ids - turn_start + SHIFT) % TURN

    def phase(ids, lags):
        steps = (ids[:, None] * lags[None, :]) % (2 * bins)
        return (steps.astype(np.float32) * np.float32(math.pi / bins)).astype(np.float64)

    cosine = np.cos(phase(bin_ids, np.arange(HALF)))
    sine = -np.sin(phase(moved, np.arange(HALF)))
    sine[:, :1] = np.cos(phase(bin_ids, np.array([HALF])))
    joined = np.concatenate([cosine, sine], axis=1)
    return joined.astype(np.float32).astype(ml_dtypes.bfloat16)


def moved_on(block):
    parts = []
    for start in range(0, block.shape[1], TURN):
        parts.append(block[:, start + SHIFT : start + TURN])
        parts.append(block[:, start : start + SHIFT])
    return jnp.concatenate(parts, axis=1)


def cross_rows(lead, tail):
    lead = lead.astype(F32)
    tail = tail.astype(F32)
    tail_re, tail_im = tail[:CH], tail[CH:]
    real, imag = [], []
    for a in range(CH):
        lead_re, lead_im = lead[a : a + 1], lead[CH + a : CH + a + 1]
        real.append(lead_re * tail_re + lead_im * tail_im)
        imag.append(lead_im * tail_re - lead_re * tail_im)
    real = jnp.concatenate(real, axis=0).astype(BF16)
    imag = jnp.concatenate(imag, axis=0).astype(BF16)
    return jnp.concatenate([real, moved_on(imag)], axis=0)


def folded(acc):
    real, imag = acc[: CH * CH, :], acc[CH * CH :, :]
    lane = lax.broadcasted_iota(jnp.int32, (CH * CH, HALF), 1)
    right = imag[:, HALF:] + jnp.where(lane == 0, real[:, HALF:], 0.0)
    return jnp.concatenate([real[:, :HALF], right], axis=1)


def kernel(
    n_pairs, n_tm, norm_scale,
    spectra, slot_hbm, tiles_hbm, owners_hbm, table_hbm,
    out,
    slot, tiles, owners, raw, own, beside, table,
    diag_acc, side_acc, diag_out, diag_in, hop_out, hop_in,
    side_out, arrived, mixed, moved_lead, moved_tail,
    index_sem, raw_sem, table_sem, send_sem, recv_sem, diag_send, diag_recv,
    hop_send, hop_recv, own_send, near_send, arrived_sem, moved_send, moved_recv,
):
    bins = own.shape[1]
    steps = bins // STEP
    here = lax.axis_index("pairs")
    window = lax.axis_index("tm")
    odd = lax.rem(window, 2)
    even_window = odd == 0
    right = lax.rem(here + 1, n_pairs)
    left = lax.rem(here + n_pairs - 1, n_pairs)
    near = lax.rem(here + 1 - 2 * odd + n_pairs, n_pairs)
    away = lax.rem(here - 1 + 2 * odd + n_pairs, n_pairs)
    to_right = lax.min(n_pairs - 1 - here, 1)
    to_left = lax.min(here, 1)
    has_right = to_right == 1
    has_left = to_left == 1
    to_near = to_right * (1 - odd) + to_left * odd
    to_away = to_left * (1 - odd) + to_right * odd
    has_near = to_near == 1
    has_away = to_away == 1
    gives_own = has_left
    starts_row = to_left * (1 - lax.min(lax.rem(here, ROW), 1))
    ends_row = to_right * (1 - lax.min(ROW - 1 - lax.rem(here, ROW), 1))
    gives_tail = starts_row * (1 - odd) == 1
    gives_lead = ends_row * (1 - odd) == 1
    takes_moved = starts_row * odd == 1
    gives_near = has_near & (here * odd != 1)

    def peer(k):
        return lax.rem(window + k, n_tm)

    barrier = pltpu.get_barrier_semaphore()

    def greet(block, t):
        pl.semaphore_signal(barrier, inc=1, device_id=(block, t), device_id_type=MESH)

    @pl.when(has_right)
    def _():
        greet(right, window)

    @pl.when(has_left)
    def _():
        greet(left, window)

    @pl.when(takes_moved)
    def _():
        greet(left, window - 1)

    far_first = sorted(range(1, n_tm), key=lambda k: abs(k - n_tm // 2))
    for k in far_first:
        greet(here, peer(k))

    def lanes(index):
        return pl.ds(pl.multiple_of(index * STEP, STEP), STEP)

    def raw_copy(part):
        return pltpu.make_async_copy(
            spectra.at[:, :, lanes(part)], raw[part], raw_sem.at[part]
        )

    def table_copy(part):
        return pltpu.make_async_copy(
            table_hbm.at[lanes(part), :], table.at[lanes(part), :], table_sem.at[part]
        )

    index_copies = [
        pltpu.make_async_copy(source, target, index_sem.at[place])
        for place, (source, target) in enumerate(
            [(slot_hbm, slot), (tiles_hbm, tiles), (owners_hbm, owners)]
        )
    ]
    index_copies[0].start()
    for part in range(steps):
        raw_copy(part).start()
    for copy in index_copies[1:]:
        copy.start()
    def block_copy(span, place):
        return pltpu.make_async_remote_copy(
            own.at[:, span], beside.at[:, span], send_sem.at[0], recv_sem.at[place],
            device_id=(away, window), device_id_type=MESH,
        )

    kept = bins - MOVED
    pieces = [
        (pl.ds(start, PIECE), steps - 2 + i)
        for i, start in enumerate(range(bins - 2 * STEP, bins, PIECE))
    ]
    moved_span = pl.ds(kept, MOVED)
    tail_copy = pltpu.make_async_remote_copy(
        own.at[:, moved_span], moved_tail, moved_send.at[0], moved_recv.at[0],
        device_id=(here, lax.rem(window + 1, n_tm)), device_id_type=MESH,
    )
    lead_copy = pltpu.make_async_remote_copy(
        own.at[:, moved_span], moved_lead, moved_send.at[0], moved_recv.at[1],
        device_id=(right, lax.rem(window + 1, n_tm)), device_id_type=MESH,
    )

    index_copies[0].wait()
    rows = [slot[c] for c in range(CH)]
    entered = 1
    for part in range(steps):
        raw_copy(part).wait()

        @pl.loop(0, STEP // 1024)
        def _(piece, part=part):
            offset = pl.multiple_of(piece * 1024, 1024)
            values = [raw[part][row, :, pl.ds(offset, 1024)].astype(F32) for row in rows]
            planar = [v[:1] for v in values] + [v[1:] for v in values]
            own[:, pl.ds(pl.multiple_of(part * STEP + offset, 1024), 1024)] = jnp.concatenate(
                planar, axis=0
            ).astype(BF16)

        if part == entered:
            pl.semaphore_wait(
                barrier, n_tm - 1 + to_left + to_right + ends_row * (1 - odd)
            )
        if entered <= part < steps - 2:

            @pl.when(has_away)
            def _(part=part):
                for ready in range(0 if part == entered else part, part + 1):
                    block_copy(lanes(ready), ready).start()

        if part >= steps - 2:
            for span, place in pieces[2 * (part - steps + 2) :][:2]:
                needed = has_away if span.start < kept else has_away & ~gives_tail

                @pl.when(needed)
                def _(span=span, place=place):
                    block_copy(span, place).start()

    @pl.when(gives_tail)
    def _():
        tail_copy.start()

    @pl.when(gives_lead)
    def _():
        lead_copy.start()

    for part in range(steps):
        table_copy(part).start()

    diag_acc[...] = jnp.zeros_like(diag_acc)
    side_acc[...] = jnp.zeros_like(side_acc)

    @pl.loop(0, steps)
    def _(part):
        table_copy(part).wait()
        block = own[:, lanes(part)]
        diag_acc[...] += jnp.dot(
            cross_rows(block, block), table[lanes(part), :], preferred_element_type=F32
        )

    def diag_copy(k):
        return pltpu.make_async_remote_copy(
            diag_out.at[peer(k)], diag_in.at[k - 1], diag_send.at[0], diag_recv.at[0],
            device_id=(here, peer(k)), device_id_type=MESH,
        )

    diag_all = pltpu.make_async_remote_copy(
        diag_out.at[pl.ds(0, n_tm - 1)], diag_in, diag_send.at[0], diag_recv.at[0],
        device_id=(here, peer(1)), device_id_type=MESH,
    )
    diag = folded(diag_acc[...])
    for t in range(n_tm):
        diag_out[t] = diag[t * CH : (t + 1) * CH]
    for k in far_first:
        diag_copy(k).start()

    for copy in index_copies[1:]:
        copy.wait()

    def next_tile(p, carry):
        count, kinds = carry[0], carry[1:]
        mine = owners[p] == here
        kind = 2 * (tiles[0, p] - here + 1) + tiles[1, p] - tiles[0, p]
        kinds = [
            jnp.where(mine & (count == s), kind, kinds[s]) for s in range(TILE_CAP)
        ]
        return (count + mine.astype(jnp.int32), *kinds)

    carry = (jnp.int32(0),) + (jnp.int32(-1),) * TILE_CAP
    kinds = lax.fori_loop(0, tiles.shape[1], next_tile, carry)[1:]

    def chosen(s, kind, tile):
        return jnp.where(kinds[s] == kind, tile, 0.0)

    def side_sum(lead, tail, span):
        side_acc[...] += jnp.dot(
            cross_rows(lead, tail), table[span, :], preferred_element_type=F32
        )

    def side_step(span, place):
        block_copy(span, place).wait_recv()
        mine = own[:, span].astype(F32)
        other = beside[:, span].astype(F32)
        side_sum(
            jnp.where(even_window, mine, other), jnp.where(even_window, other, mine), span
        )

    hop = pltpu.make_async_remote_copy(
        hop_out, hop_in, hop_send.at[0], hop_recv.at[0],
        device_id=(right, window), device_id_type=MESH,
    )

    @pl.loop(0, steps - 2)
    def _(part):
        @pl.when(has_near)
        def _():
            side_step(lanes(part), part)

    diag_all.wait_recv()
    diag_sum = diag_out[window]
    for k in range(n_tm - 1):
        diag_sum += diag_in[k]
    hop_out[...] = diag_sum

    @pl.when(has_right)
    def _():
        hop.start()

    @pl.when(takes_moved)
    def _():
        tail_copy.wait_recv()
        lead_copy.wait_recv()
        for start in range(0, MOVED, PIECE):
            part = pl.ds(start, PIECE)
            side_sum(moved_lead[:, part], moved_tail[:, part], pl.ds(kept + start, PIECE))

    for span, place in pieces:
        needed = has_near if span.start < kept else has_near & ~gives_lead

        @pl.when(needed)
        def _(span=span, place=place):
            side_step(span, place)

    def own_copy(k):
        return pltpu.make_async_remote_copy(
            side_out.at[peer(k)], arrived.at[window], own_send.at[0], arrived_sem.at[0],
            device_id=(here, peer(k)), device_id_type=MESH,
        )

    def right_copy(k):
        return pltpu.make_async_remote_copy(
            side_out.at[peer(k)], arrived.at[n_tm + window // 2],
            near_send.at[0], arrived_sem.at[0],
            device_id=(right, peer(k)), device_id_type=MESH,
        )

    def left_copy(k):
        return pltpu.make_async_remote_copy(
            side_out.at[peer(k)], arrived.at[n_tm + n_tm // 2 + window // 2],
            near_send.at[0], arrived_sem.at[0],
            device_id=(left, peer(k)), device_id_type=MESH,
        )

    def several(buffer, count, send):
        return pltpu.make_async_remote_copy(
            buffer.at[pl.ds(0, count)], buffer.at[pl.ds(0, count)], send, arrived_sem.at[0],
            device_id=(right, window), device_id_type=MESH,
        )

    side = folded(side_acc[...])
    for t in range(n_tm):
        side_out[t] = side[t * CH : (t + 1) * CH]

    @pl.when(gives_near)
    def _():
        @pl.when(even_window)
        def _():
            for k in far_first + [0]:
                right_copy(k).start()

        @pl.when(odd == 1)
        def _():
            for k in far_first + [0]:
                left_copy(k).start()

    @pl.when(gives_own)
    def _():
        for k in far_first:
            own_copy(k).start()

    arrived[window] = side_out[window]
    for s in range(TILE_CAP):
        mixed[s] = chosen(s, 2, diag_sum)

    def sent(span):
        pltpu.make_async_remote_copy(
            own.at[:, span], beside.at[:, span], send_sem.at[0], recv_sem.at[0],
            device_id=(away, window), device_id_type=MESH,
        ).wait_send()

    @pl.when(has_away & ~gives_tail)
    def _():
        sent(pl.ds(0, bins))

    @pl.when(gives_tail)
    def _():
        sent(pl.ds(0, kept))
        tail_copy.wait_send()

    @pl.when(gives_lead)
    def _():
        lead_copy.wait_send()

    diag_all.wait_send()

    @pl.when(has_right)
    def _():
        hop.wait_send()

    @pl.when(has_left)
    def _():
        hop.wait_recv()
        for s in range(TILE_CAP):
            mixed[s] += chosen(s, 0, hop_in[...])

    @pl.when(has_left & has_right)
    def _():
        several(arrived, 2 * n_tm - 1, own_send.at[0]).wait_recv()
        after = arrived[0]
        for place in range(2, n_tm, 2):
            after += arrived[place]
        for place in range(n_tm + n_tm // 2, 2 * n_tm):
            after += arrived[place]
        for s in range(TILE_CAP):
            mixed[s] += chosen(s, 3, after)

    @pl.when(has_left & (to_right == 0))
    def _():
        several(arrived, n_tm - 1 + n_tm // 2, own_send.at[0]).wait_recv()

    @pl.when(has_left)
    def _():
        before = arrived[1]
        for place in range(3, n_tm, 2):
            before += arrived[place]
        for place in range(n_tm, n_tm + n_tm // 2):
            before += arrived[place]
        for s in range(TILE_CAP):
            mixed[s] += chosen(s, 1, before)

    lane = lax.broadcasted_iota(jnp.int32, (CH, HALF), 1)
    mirror = lax.rem(HALF - lane, HALF)
    for s in range(TILE_CAP):
        cosine, sine = mixed[s, :, :HALF], mixed[s, :, HALF:]
        before = jnp.where(lane == 0, sine, cosine - sine)
        before = jnp.take_along_axis(before, mirror, axis=1)
        after = jnp.where(lane == 0, cosine, cosine + sine)
        out[s] = jnp.concatenate([before, after], axis=1) * norm_scale

    @pl.when(gives_near)
    def _():
        several(arrived, n_tm, near_send.at[0]).wait_send()

    @pl.when(gives_own)
    def _():
        several(arrived, n_tm - 1, own_send.at[0]).wait_send()


def on_device(n_pairs, n_tm, spectra, channel_slot, tile_list, tile_owner):
    bins = spectra.shape[3]
    steps = bins // STEP
    dma = pltpu.SemaphoreType.DMA
    vmem = pl.BlockSpec(memory_space=pltpu.VMEM)
    hbm = pl.BlockSpec(memory_space=pl.ANY)
    group = pltpu.VMEM((n_tm, CH, LAGS), F32)
    share = pltpu.VMEM((CH, LAGS), F32)
    return pl.pallas_call(
        functools.partial(kernel, n_pairs, n_tm, 1.0 / math.sqrt(2.0 * bins * n_tm)),
        out_shape=jax.ShapeDtypeStruct((TILE_CAP, CH, LAGS), F32),
        in_specs=[hbm] * 5,
        out_specs=vmem,
        scratch_shapes=[
            pltpu.SMEM(channel_slot.shape, jnp.int32),
            pltpu.SMEM(tile_list.shape[::-1], jnp.int32),
            pltpu.SMEM(tile_owner.shape, jnp.int32),
            [pltpu.VMEM((CH, 2, STEP), BF16) for _ in range(steps)],
            pltpu.VMEM((2 * CH, bins), BF16),
            pltpu.VMEM((2 * CH, bins), BF16),
            pltpu.VMEM((bins, LAGS), BF16),
            pltpu.VMEM((2 * CH * CH, LAGS), F32),
            pltpu.VMEM((2 * CH * CH, LAGS), F32),
            group,
            pltpu.VMEM((n_tm - 1, CH, LAGS), F32),
            share,
            share,
            group,
            pltpu.VMEM((2 * n_tm, CH, LAGS), F32),
            pltpu.VMEM((TILE_CAP, CH, LAGS), F32),
            pltpu.VMEM((2 * CH, MOVED), BF16),
            pltpu.VMEM((2 * CH, MOVED), BF16),
            dma((3,)),
            dma((steps,)),
            dma((steps,)),
            dma((1,)),
            dma((steps + 2,)),
            dma((1,)),
            dma((1,)),
            dma((1,)),
            dma((1,)),
            dma((1,)),
            dma((1,)),
            dma((1,)),
            dma((1,)),
            dma((2,)),
        ],
        compiler_params=pltpu.CompilerParams(
            collective_id=0, has_side_effects=True, vmem_limit_bytes=48 * 1024 * 1024
        ),
    )(
        *(
            pltpu.with_memory_space_constraint(operand, pltpu.HBM)
            for operand in (
                spectra[0], channel_slot, tile_list.T, tile_owner, jnp.asarray(lag_table(bins))
            )
        )
    )


def solution(mesh):
    placed = (P("tm", "pairs", None, None), P("pairs"), P(), P())
    body = functools.partial(on_device, mesh.shape["pairs"], mesh.shape["tm"])
    return jax.shard_map(
        body, mesh=mesh, in_specs=placed, out_specs=P("pairs", "tm", None), check_vma=False
    )
```

```python
import functools
import math

import jax
import jax.numpy as jnp
import ml_dtypes
import numpy as np
from jax import lax
from jax.experimental import pallas as pl
from jax.experimental.pallas import tpu as pltpu
from jax.sharding import PartitionSpec as P

LAGS = 256
TILE_CAP = 4
CH = 8
HALF = LAGS // 2
TURN = 512
SHIFT = TURN // 4
STEP = 4096
MESH = pl.DeviceIdType.MESH
F32 = jnp.float32
BF16 = jnp.bfloat16


def lag_table(bins):
    bin_ids = np.arange(bins)
    turn_start = bin_ids // TURN * TURN
    moved = turn_start + (bin_ids - turn_start + SHIFT) % TURN

    def phase(ids, lags):
        steps = (ids[:, None] * lags[None, :]) % (2 * bins)
        return (steps.astype(np.float32) * np.float32(math.pi / bins)).astype(np.float64)

    cosine = np.cos(phase(bin_ids, np.arange(HALF)))
    sine = -np.sin(phase(moved, np.arange(HALF)))
    sine[:, :1] = np.cos(phase(bin_ids, np.array([HALF])))
    joined = np.concatenate([cosine, sine], axis=1)
    return joined.astype(np.float32).astype(ml_dtypes.bfloat16)


def moved_on(block):
    parts = []
    for start in range(0, block.shape[1], TURN):
        parts.append(block[:, start + SHIFT : start + TURN])
        parts.append(block[:, start : start + SHIFT])
    return jnp.concatenate(parts, axis=1)


def cross_rows(lead, tail):
    lead = lead.astype(F32)
    tail = tail.astype(F32)
    tail_re, tail_im = tail[:CH], tail[CH:]
    real, imag = [], []
    for a in range(CH):
        lead_re, lead_im = lead[a : a + 1], lead[CH + a : CH + a + 1]
        real.append(lead_re * tail_re + lead_im * tail_im)
        imag.append(lead_im * tail_re - lead_re * tail_im)
    real = jnp.concatenate(real, axis=0).astype(BF16)
    imag = jnp.concatenate(imag, axis=0).astype(BF16)
    return jnp.concatenate([real, moved_on(imag)], axis=0)


def folded(acc):
    real, imag = acc[: CH * CH, :], acc[CH * CH :, :]
    lane = lax.broadcasted_iota(jnp.int32, (CH * CH, HALF), 1)
    right = imag[:, HALF:] + jnp.where(lane == 0, real[:, HALF:], 0.0)
    return jnp.concatenate([real[:, :HALF], right], axis=1)


def kernel(
    n_pairs, n_tm, norm_scale,
    spectra, slot_hbm, tiles_hbm, owners_hbm, table_hbm,
    out,
    slot, tiles, owners, raw, own, beside, table,
    diag_acc, side_acc, diag_out, diag_in, hop_out, hop_in,
    side_out, arrived, mixed,
    index_sem, raw_sem, table_sem, send_sem, recv_sem, diag_send, diag_recv,
    hop_send, hop_recv, own_send, near_send, arrived_sem, ready,
):
    bins = own.shape[1]
    steps = bins // STEP
    here = lax.axis_index("pairs")
    window = lax.axis_index("tm")
    odd = 1 - lax.rem(window, 2)
    even_window = odd == 0
    right = lax.rem(here + 1, n_pairs)
    left = lax.rem(here + n_pairs - 1, n_pairs)
    near = lax.rem(here + 1 - 2 * odd + n_pairs, n_pairs)
    away = lax.rem(here - 1 + 2 * odd + n_pairs, n_pairs)
    to_right = lax.min(n_pairs - 1 - here, 1)
    to_left = lax.min(here, 1)
    has_right = to_right == 1
    has_left = to_left == 1
    to_near = to_right * (1 - odd) + to_left * odd
    to_away = to_left * (1 - odd) + to_right * odd
    has_near = to_near == 1
    has_away = to_away == 1
    gives_own = has_left
    gives_near = has_near & (here * odd != 1)

    def peer(k):
        return lax.rem(window + k, n_tm)

    barrier = pltpu.get_barrier_semaphore()

    def greet(block, t):
        pl.semaphore_signal(barrier, inc=1, device_id=(block, t), device_id_type=MESH)

    @pl.when(has_near)
    def _():
        greet(near, window)

    far_first = sorted(range(1, n_tm), key=lambda k: abs(k - n_tm // 2))
    core = lax.rem(window, 2)
    first = window - core
    others = [lax.rem(first + 2 * dx + n_tm, n_tm) for dx in (-1, 1)]
    for base in others:
        for t in range(2):
            greet(here, base + t)
    greet(here, first + 1 - core)

    def lanes(index):
        return pl.ds(pl.multiple_of(index * STEP, STEP), STEP)

    def raw_copy(part):
        return pltpu.make_async_copy(
            spectra.at[:, :, lanes(part)], raw[part], raw_sem.at[part]
        )

    def table_copy(part):
        return pltpu.make_async_copy(
            table_hbm.at[lanes(part), :], table.at[lanes(part), :], table_sem.at[part]
        )

    index_copies = [
        pltpu.make_async_copy(source, target, index_sem.at[place])
        for place, (source, target) in enumerate(
            [(slot_hbm, slot), (tiles_hbm, tiles), (owners_hbm, owners)]
        )
    ]
    index_copies[0].start()
    for part in range(steps):
        raw_copy(part).start()
    for copy in index_copies[1:]:
        copy.start()
    def block_copy(span, place):
        return pltpu.make_async_remote_copy(
            own.at[:, span], beside.at[:, span], send_sem.at[0], recv_sem.at[place],
            device_id=(away, window), device_id_type=MESH,
        )

    last = [
        (pl.ds((steps - 1) * STEP + i * STEP // 2, STEP // 2), steps - 1 + i) for i in range(2)
    ]

    index_copies[0].wait()
    rows = [slot[c] for c in range(CH)]
    entered = 1
    for part in range(steps):
        raw_copy(part).wait()

        @pl.loop(0, STEP // 1024)
        def _(piece, part=part):
            offset = pl.multiple_of(piece * 1024, 1024)
            values = [raw[part][row, :, pl.ds(offset, 1024)].astype(F32) for row in rows]
            planar = [v[:1] for v in values] + [v[1:] for v in values]
            own[:, pl.ds(pl.multiple_of(part * STEP + offset, 1024), 1024)] = jnp.concatenate(
                planar, axis=0
            ).astype(BF16)

        if part == entered:
            pl.semaphore_wait(barrier, 5 + to_away)
            pl.semaphore_signal(
                ready, inc=1, device_id=(here, others[0] + core), device_id_type=MESH
            )
        if entered <= part < steps - 1:

            @pl.when(has_away)
            def _(part=part):
                for sent in range(0 if part == entered else part, part + 1):
                    block_copy(lanes(sent), sent).start()

    pl.semaphore_wait(ready, 1)

    @pl.when(has_away)
    def _():
        for span, place in last:
            block_copy(span, place).start()

    for part in range(steps):
        table_copy(part).start()

    diag_acc[...] = jnp.zeros_like(diag_acc)
    side_acc[...] = jnp.zeros_like(side_acc)

    @pl.loop(0, steps)
    def _(part):
        table_copy(part).wait()
        block = own[:, lanes(part)]
        diag_acc[...] += jnp.dot(
            cross_rows(block, block), table[lanes(part), :], preferred_element_type=F32
        )

    def diag_copy(k):
        return pltpu.make_async_remote_copy(
            diag_out.at[peer(k)], diag_in.at[k - 1], diag_send.at[0], diag_recv.at[0],
            device_id=(here, peer(k)), device_id_type=MESH,
        )

    diag_all = pltpu.make_async_remote_copy(
        diag_out.at[pl.ds(0, n_tm - 1)], diag_in, diag_send.at[0], diag_recv.at[0],
        device_id=(here, peer(1)), device_id_type=MESH,
    )
    diag = folded(diag_acc[...])
    for t in range(n_tm):
        diag_out[t] = diag[t * CH : (t + 1) * CH]
    for k in far_first:
        diag_copy(k).start()

    for copy in index_copies[1:]:
        copy.wait()

    def next_tile(p, carry):
        count, kinds = carry[0], carry[1:]
        mine = owners[p] == here
        kind = 2 * (tiles[0, p] - here + 1) + tiles[1, p] - tiles[0, p]
        kinds = [
            jnp.where(mine & (count == s), kind, kinds[s]) for s in range(TILE_CAP)
        ]
        return (count + mine.astype(jnp.int32), *kinds)

    carry = (jnp.int32(0),) + (jnp.int32(-1),) * TILE_CAP
    kinds = lax.fori_loop(0, tiles.shape[1], next_tile, carry)[1:]

    def chosen(s, kind, tile):
        return jnp.where(kinds[s] == kind, tile, 0.0)

    def side_step(span, place):
        block_copy(span, place).wait_recv()
        mine = own[:, span].astype(F32)
        other = beside[:, span].astype(F32)
        lead = jnp.where(even_window, mine, other)
        tail = jnp.where(even_window, other, mine)
        side_acc[...] += jnp.dot(
            cross_rows(lead, tail), table[span, :], preferred_element_type=F32
        )

    hop = pltpu.make_async_remote_copy(
        hop_out, hop_in, hop_send.at[0], hop_recv.at[0],
        device_id=(right, window), device_id_type=MESH,
    )

    @pl.loop(0, steps - 2)
    def _(part):
        @pl.when(has_near)
        def _():
            side_step(lanes(part), part)

    diag_all.wait_recv()
    diag_sum = diag_out[window]
    for k in range(n_tm - 1):
        diag_sum += diag_in[k]
    hop_out[...] = diag_sum

    @pl.when(has_right)
    def _():
        hop.start()

    @pl.when(has_near)
    def _():
        side_step(lanes(steps - 2), steps - 2)
        for span, place in last:
            side_step(span, place)

    def own_copy(k):
        return pltpu.make_async_remote_copy(
            side_out.at[peer(k)], arrived.at[window], own_send.at[0], arrived_sem.at[0],
            device_id=(here, peer(k)), device_id_type=MESH,
        )

    def right_copy(k):
        return pltpu.make_async_remote_copy(
            side_out.at[peer(k)], arrived.at[n_tm + window // 2],
            near_send.at[0], arrived_sem.at[0],
            device_id=(right, peer(k)), device_id_type=MESH,
        )

    def left_copy(k):
        return pltpu.make_async_remote_copy(
            side_out.at[peer(k)], arrived.at[n_tm + n_tm // 2 + window // 2],
            near_send.at[0], arrived_sem.at[0],
            device_id=(left, peer(k)), device_id_type=MESH,
        )

    def several(buffer, count, send):
        return pltpu.make_async_remote_copy(
            buffer.at[pl.ds(0, count)], buffer.at[pl.ds(0, count)], send, arrived_sem.at[0],
            device_id=(right, window), device_id_type=MESH,
        )

    side = folded(side_acc[...])
    for t in range(n_tm):
        side_out[t] = side[t * CH : (t + 1) * CH]

    @pl.when(gives_near)
    def _():
        @pl.when(even_window)
        def _():
            for k in far_first + [0]:
                right_copy(k).start()

        @pl.when(odd == 1)
        def _():
            for k in far_first + [0]:
                left_copy(k).start()

    @pl.when(gives_own)
    def _():
        for k in far_first:
            own_copy(k).start()

    arrived[window] = side_out[window]
    for s in range(TILE_CAP):
        mixed[s] = chosen(s, 2, diag_sum)

    @pl.when(has_away)
    def _():
        pltpu.make_async_remote_copy(
            own, beside, send_sem.at[0], recv_sem.at[0],
            device_id=(away, window), device_id_type=MESH,
        ).wait_send()

    diag_all.wait_send()

    @pl.when(has_right)
    def _():
        hop.wait_send()

    @pl.when(has_left)
    def _():
        hop.wait_recv()
        for s in range(TILE_CAP):
            mixed[s] += chosen(s, 0, hop_in[...])

    @pl.when(has_left & has_right)
    def _():
        several(arrived, 2 * n_tm - 1, own_send.at[0]).wait_recv()
        after = arrived[1]
        for place in range(3, n_tm, 2):
            after += arrived[place]
        for place in range(n_tm + n_tm // 2, 2 * n_tm):
            after += arrived[place]
        for s in range(TILE_CAP):
            mixed[s] += chosen(s, 3, after)

    @pl.when(has_left & (to_right == 0))
    def _():
        several(arrived, n_tm - 1 + n_tm // 2, own_send.at[0]).wait_recv()

    @pl.when(has_left)
    def _():
        before = arrived[0]
        for place in range(2, n_tm, 2):
            before += arrived[place]
        for place in range(n_tm, n_tm + n_tm // 2):
            before += arrived[place]
        for s in range(TILE_CAP):
            mixed[s] += chosen(s, 1, before)

    lane = lax.broadcasted_iota(jnp.int32, (CH, HALF), 1)
    mirror = lax.rem(HALF - lane, HALF)
    for s in range(TILE_CAP):
        cosine, sine = mixed[s, :, :HALF], mixed[s, :, HALF:]
        before = jnp.where(lane == 0, sine, cosine - sine)
        before = jnp.take_along_axis(before, mirror, axis=1)
        after = jnp.where(lane == 0, cosine, cosine + sine)
        out[s] = jnp.concatenate([before, after], axis=1) * norm_scale

    @pl.when(gives_near)
    def _():
        several(arrived, n_tm, near_send.at[0]).wait_send()

    @pl.when(gives_own)
    def _():
        several(arrived, n_tm - 1, own_send.at[0]).wait_send()


def on_device(n_pairs, n_tm, spectra, channel_slot, tile_list, tile_owner):
    bins = spectra.shape[3]
    steps = bins // STEP
    dma = pltpu.SemaphoreType.DMA
    vmem = pl.BlockSpec(memory_space=pltpu.VMEM)
    hbm = pl.BlockSpec(memory_space=pl.ANY)
    group = pltpu.VMEM((n_tm, CH, LAGS), F32)
    share = pltpu.VMEM((CH, LAGS), F32)
    return pl.pallas_call(
        functools.partial(kernel, n_pairs, n_tm, 1.0 / math.sqrt(2.0 * bins * n_tm)),
        out_shape=jax.ShapeDtypeStruct((TILE_CAP, CH, LAGS), F32),
        in_specs=[hbm] * 5,
        out_specs=vmem,
        scratch_shapes=[
            pltpu.SMEM(channel_slot.shape, jnp.int32),
            pltpu.SMEM(tile_list.shape[::-1], jnp.int32),
            pltpu.SMEM(tile_owner.shape, jnp.int32),
            [pltpu.VMEM((CH, 2, STEP), BF16) for _ in range(steps)],
            pltpu.VMEM((2 * CH, bins), BF16),
            pltpu.VMEM((2 * CH, bins), BF16),
            pltpu.VMEM((bins, LAGS), BF16),
            pltpu.VMEM((2 * CH * CH, LAGS), F32),
            pltpu.VMEM((2 * CH * CH, LAGS), F32),
            group,
            pltpu.VMEM((n_tm - 1, CH, LAGS), F32),
            share,
            share,
            group,
            pltpu.VMEM((2 * n_tm, CH, LAGS), F32),
            pltpu.VMEM((TILE_CAP, CH, LAGS), F32),
            dma((3,)),
            dma((steps,)),
            dma((steps,)),
            dma((1,)),
            dma((steps + 1,)),
            dma((1,)),
            dma((1,)),
            dma((1,)),
            dma((1,)),
            dma((1,)),
            dma((1,)),
            dma((1,)),
            pltpu.SemaphoreType.REGULAR,
        ],
        compiler_params=pltpu.CompilerParams(
            collective_id=0, has_side_effects=True, vmem_limit_bytes=48 * 1024 * 1024
        ),
    )(
        *(
            pltpu.with_memory_space_constraint(operand, pltpu.HBM)
            for operand in (
                spectra[0], channel_slot, tile_list.T, tile_owner, jnp.asarray(lag_table(bins))
            )
        )
    )


def solution(mesh):
    placed = (P("tm", "pairs", None, None), P("pairs"), P(), P())
    body = functools.partial(on_device, mesh.shape["pairs"], mesh.shape["tm"])
    return jax.shard_map(
        body, mesh=mesh, in_specs=placed, out_specs=P("pairs", "tm", None), check_vma=False
    )
```

```python
import functools
import math

import jax
import jax.numpy as jnp
import ml_dtypes
import numpy as np
from jax import lax
from jax.experimental import pallas as pl
from jax.experimental.pallas import tpu as pltpu
from jax.sharding import PartitionSpec as P

LAGS = 256
TILE_CAP = 4
CH = 8
HALF = LAGS // 2
TURN = 512
SHIFT = TURN // 4
STEP = 4096
PIECE = STEP // 4
MESH = pl.DeviceIdType.MESH
F32 = jnp.float32
BF16 = jnp.bfloat16


def lag_table(bins):
    bin_ids = np.arange(bins)
    turn_start = bin_ids // TURN * TURN
    moved = turn_start + (bin_ids - turn_start + SHIFT) % TURN

    def phase(ids, lags):
        steps = (ids[:, None] * lags[None, :]) % (2 * bins)
        return (steps.astype(np.float32) * np.float32(math.pi / bins)).astype(np.float64)

    cosine = np.cos(phase(bin_ids, np.arange(HALF)))
    sine = -np.sin(phase(moved, np.arange(HALF)))
    sine[:, :1] = np.cos(phase(bin_ids, np.array([HALF])))
    joined = np.concatenate([cosine, sine], axis=1)
    return joined.astype(np.float32).astype(ml_dtypes.bfloat16)


def moved_on(block):
    parts = []
    for start in range(0, block.shape[1], TURN):
        parts.append(block[:, start + SHIFT : start + TURN])
        parts.append(block[:, start : start + SHIFT])
    return jnp.concatenate(parts, axis=1)


def cross_rows(lead, tail):
    lead = lead.astype(F32)
    tail = tail.astype(F32)
    tail_re, tail_im = tail[:CH], tail[CH:]
    real, imag = [], []
    for a in range(CH):
        lead_re, lead_im = lead[a : a + 1], lead[CH + a : CH + a + 1]
        real.append(lead_re * tail_re + lead_im * tail_im)
        imag.append(lead_im * tail_re - lead_re * tail_im)
    real = jnp.concatenate(real, axis=0).astype(BF16)
    imag = jnp.concatenate(imag, axis=0).astype(BF16)
    return jnp.concatenate([real, moved_on(imag)], axis=0)


def folded(acc):
    real, imag = acc[: CH * CH, :], acc[CH * CH :, :]
    lane = lax.broadcasted_iota(jnp.int32, (CH * CH, HALF), 1)
    right = imag[:, HALF:] + jnp.where(lane == 0, real[:, HALF:], 0.0)
    return jnp.concatenate([real[:, :HALF], right], axis=1)


def kernel(
    n_pairs, n_tm, norm_scale,
    spectra, slot_hbm, tiles_hbm, owners_hbm, table_hbm,
    out,
    slot, tiles, owners, raw, own, beside, table,
    diag_acc, side_acc, diag_out, diag_in, hop_out, hop_in,
    side_out, arrived, mixed,
    index_sem, raw_sem, table_sem, send_sem, recv_sem, diag_send, diag_recv,
    hop_send, hop_recv, own_send, near_send, arrived_sem, ready,
):
    bins = own.shape[1]
    steps = bins // STEP
    here = lax.axis_index("pairs")
    window = lax.axis_index("tm")
    odd = 1 - lax.rem(window, 2)
    even_window = odd == 0
    right = lax.rem(here + 1, n_pairs)
    left = lax.rem(here + n_pairs - 1, n_pairs)
    near = lax.rem(here + 1 - 2 * odd + n_pairs, n_pairs)
    away = lax.rem(here - 1 + 2 * odd + n_pairs, n_pairs)
    to_right = lax.min(n_pairs - 1 - here, 1)
    to_left = lax.min(here, 1)
    has_right = to_right == 1
    has_left = to_left == 1
    to_near = to_right * (1 - odd) + to_left * odd
    to_away = to_left * (1 - odd) + to_right * odd
    has_near = to_near == 1
    has_away = to_away == 1
    gives_own = has_left
    gives_near = has_near & (here * odd != 1)

    def peer(k):
        return lax.rem(window + k, n_tm)

    barrier = pltpu.get_barrier_semaphore()

    def greet(block, t):
        pl.semaphore_signal(barrier, inc=1, device_id=(block, t), device_id_type=MESH)

    @pl.when(has_near)
    def _():
        greet(near, window)

    core = lax.rem(window, 2)
    partner = window + 1 - 2 * core
    beside_odd = [lax.rem(window - core + 2 * dx + n_tm, n_tm) + 1 for dx in (-1, 1)]
    far_first = sorted(range(1, n_tm), key=lambda k: abs(k - n_tm // 2))
    greet(here, partner)

    @pl.when(core == 1)
    def _():
        for t in beside_odd:
            greet(here, t)

    def vouch(place, t):
        pl.semaphore_signal(
            ready.at[place], inc=1, device_id=(here, t), device_id_type=MESH
        )

    def lanes(index):
        return pl.ds(pl.multiple_of(index * STEP, STEP), STEP)

    def raw_copy(part):
        return pltpu.make_async_copy(
            spectra.at[:, :, lanes(part)], raw[part], raw_sem.at[part]
        )

    def table_copy(part):
        return pltpu.make_async_copy(
            table_hbm.at[lanes(part), :], table.at[lanes(part), :], table_sem.at[part]
        )

    index_copies = [
        pltpu.make_async_copy(source, target, index_sem.at[place])
        for place, (source, target) in enumerate(
            [(slot_hbm, slot), (tiles_hbm, tiles), (owners_hbm, owners)]
        )
    ]
    index_copies[0].start()
    for part in range(steps):
        raw_copy(part).start()
    for copy in index_copies[1:]:
        copy.start()
    def block_copy(span, place):
        return pltpu.make_async_remote_copy(
            own.at[:, span], beside.at[:, span], send_sem.at[0], recv_sem.at[place],
            device_id=(away, window), device_id_type=MESH,
        )

    last = [
        (pl.ds((steps - 1) * STEP + i * PIECE, PIECE), steps - 1 + i)
        for i in range(STEP // PIECE)
    ]

    def slot_kinds():
        for copy in index_copies[1:]:
            copy.wait()

        def next_tile(p, carry):
            count, kinds = carry[0], carry[1:]
            mine = owners[p] == here
            kind = 2 * (tiles[0, p] - here + 1) + tiles[1, p] - tiles[0, p]
            kinds = [
                jnp.where(mine & (count == s), kind, kinds[s]) for s in range(TILE_CAP)
            ]
            return (count + mine.astype(jnp.int32), *kinds)

        carry = (jnp.int32(0),) + (jnp.int32(-1),) * TILE_CAP
        return lax.fori_loop(0, tiles.shape[1], next_tile, carry)[1:]

    index_copies[0].wait()
    rows = [slot[c] for c in range(CH)]
    entered = 1
    for part in range(steps):
        if part <= entered:
            raw_copy(part).wait()

        @pl.loop(0, STEP // 1024)
        def _(piece, part=part):
            offset = pl.multiple_of(piece * 1024, 1024)
            values = [raw[part][row, :, pl.ds(offset, 1024)].astype(F32) for row in rows]
            planar = [v[:1] for v in values] + [v[1:] for v in values]
            own[:, pl.ds(pl.multiple_of(part * STEP + offset, 1024), 1024)] = jnp.concatenate(
                planar, axis=0
            ).astype(BF16)

        if part == entered:
            pl.semaphore_wait(barrier, 1 + 2 * core + to_away)

            @pl.when(core == 1)
            def _():
                for t in beside_odd:
                    vouch(0, t)

        if entered <= part < steps - 1:

            @pl.when(has_away)
            def _(part=part):
                for sent in range(0 if part == entered else part, part + 1):
                    block_copy(lanes(sent), sent).start()

        if part == entered:
            for later in range(entered + 1, steps):
                raw_copy(later).wait()
            for later in range(steps):
                table_copy(later).start()

    @pl.when(core == 1)
    def _():
        pl.semaphore_wait(ready.at[0], 2)
        vouch(1, beside_odd[0])

    diag_acc[...] = jnp.zeros_like(diag_acc)
    side_acc[...] = jnp.zeros_like(side_acc)

    @pl.loop(0, steps)
    def _(part):
        table_copy(part).wait()
        block = own[:, lanes(part)]
        diag_acc[...] += jnp.dot(
            cross_rows(block, block), table[lanes(part), :], preferred_element_type=F32
        )

    @pl.when(core == 1)
    def _():
        pl.semaphore_wait(ready.at[1], 1)
        vouch(2, partner)

    @pl.when(core == 0)
    def _():
        pl.semaphore_wait(ready.at[2], 1)

    @pl.when(has_away)
    def _():
        for span, place in last:
            block_copy(span, place).start()

    def diag_copy(k):
        return pltpu.make_async_remote_copy(
            diag_out.at[peer(k)], diag_in.at[k - 1], diag_send.at[0], diag_recv.at[0],
            device_id=(here, peer(k)), device_id_type=MESH,
        )

    diag_all = pltpu.make_async_remote_copy(
        diag_out.at[pl.ds(0, n_tm - 1)], diag_in, diag_send.at[0], diag_recv.at[0],
        device_id=(here, peer(1)), device_id_type=MESH,
    )
    diag = folded(diag_acc[...])
    for t in range(n_tm):
        diag_out[t] = diag[t * CH : (t + 1) * CH]
    for k in far_first:
        diag_copy(k).start()

    kinds = slot_kinds()

    def chosen(s, kind, tile):
        return jnp.where(kinds[s] == kind, tile, 0.0)

    def side_step(span, place):
        block_copy(span, place).wait_recv()
        mine = own[:, span].astype(F32)
        other = beside[:, span].astype(F32)
        lead = jnp.where(even_window, mine, other)
        tail = jnp.where(even_window, other, mine)
        side_acc[...] += jnp.dot(
            cross_rows(lead, tail), table[span, :], preferred_element_type=F32
        )

    hop = pltpu.make_async_remote_copy(
        hop_out, hop_in, hop_send.at[0], hop_recv.at[0],
        device_id=(right, window), device_id_type=MESH,
    )

    @pl.loop(0, steps - 2)
    def _(part):
        @pl.when(has_near)
        def _():
            side_step(lanes(part), part)

    diag_all.wait_recv()
    diag_sum = diag_out[window]
    for k in range(n_tm - 1):
        diag_sum += diag_in[k]
    hop_out[...] = diag_sum

    @pl.when(has_right)
    def _():
        hop.start()

    @pl.when(has_near)
    def _():
        side_step(lanes(steps - 2), steps - 2)
        for span, place in last:
            side_step(span, place)

    def own_copy(k):
        return pltpu.make_async_remote_copy(
            side_out.at[peer(k)], arrived.at[window], own_send.at[0], arrived_sem.at[0],
            device_id=(here, peer(k)), device_id_type=MESH,
        )

    def right_copy(k):
        return pltpu.make_async_remote_copy(
            side_out.at[peer(k)], arrived.at[n_tm + window // 2],
            near_send.at[0], arrived_sem.at[0],
            device_id=(right, peer(k)), device_id_type=MESH,
        )

    def left_copy(k):
        return pltpu.make_async_remote_copy(
            side_out.at[peer(k)], arrived.at[n_tm + n_tm // 2 + window // 2],
            near_send.at[0], arrived_sem.at[0],
            device_id=(left, peer(k)), device_id_type=MESH,
        )

    def several(buffer, count, send):
        return pltpu.make_async_remote_copy(
            buffer.at[pl.ds(0, count)], buffer.at[pl.ds(0, count)], send, arrived_sem.at[0],
            device_id=(right, window), device_id_type=MESH,
        )

    side = folded(side_acc[...])
    for t in range(n_tm):
        side_out[t] = side[t * CH : (t + 1) * CH]

    @pl.when(gives_near)
    def _():
        @pl.when(even_window)
        def _():
            for k in far_first + [0]:
                right_copy(k).start()

        @pl.when(odd == 1)
        def _():
            for k in far_first + [0]:
                left_copy(k).start()

    @pl.when(gives_own)
    def _():
        for k in far_first:
            own_copy(k).start()

    arrived[window] = side_out[window]
    for s in range(TILE_CAP):
        mixed[s] = chosen(s, 2, diag_sum)

    @pl.when(has_away)
    def _():
        pltpu.make_async_remote_copy(
            own, beside, send_sem.at[0], recv_sem.at[0],
            device_id=(away, window), device_id_type=MESH,
        ).wait_send()

    diag_all.wait_send()

    @pl.when(has_right)
    def _():
        hop.wait_send()

    @pl.when(has_left)
    def _():
        hop.wait_recv()
        for s in range(TILE_CAP):
            mixed[s] += chosen(s, 0, hop_in[...])

    @pl.when(has_left & has_right)
    def _():
        several(arrived, 2 * n_tm - 1, own_send.at[0]).wait_recv()
        after = arrived[1]
        for place in range(3, n_tm, 2):
            after += arrived[place]
        for place in range(n_tm + n_tm // 2, 2 * n_tm):
            after += arrived[place]
        for s in range(TILE_CAP):
            mixed[s] += chosen(s, 3, after)

    @pl.when(has_left & (to_right == 0))
    def _():
        several(arrived, n_tm - 1 + n_tm // 2, own_send.at[0]).wait_recv()

    @pl.when(has_left)
    def _():
        before = arrived[0]
        for place in range(2, n_tm, 2):
            before += arrived[place]
        for place in range(n_tm, n_tm + n_tm // 2):
            before += arrived[place]
        for s in range(TILE_CAP):
            mixed[s] += chosen(s, 1, before)

    lane = lax.broadcasted_iota(jnp.int32, (CH, HALF), 1)
    mirror = lax.rem(HALF - lane, HALF)
    for s in range(TILE_CAP):
        cosine, sine = mixed[s, :, :HALF], mixed[s, :, HALF:]
        before = jnp.where(lane == 0, sine, cosine - sine)
        before = jnp.take_along_axis(before, mirror, axis=1)
        after = jnp.where(lane == 0, cosine, cosine + sine)
        out[s] = jnp.concatenate([before, after], axis=1) * norm_scale

    @pl.when(gives_near)
    def _():
        several(arrived, n_tm, near_send.at[0]).wait_send()

    @pl.when(gives_own)
    def _():
        several(arrived, n_tm - 1, own_send.at[0]).wait_send()


def on_device(n_pairs, n_tm, spectra, channel_slot, tile_list, tile_owner):
    bins = spectra.shape[3]
    steps = bins // STEP
    dma = pltpu.SemaphoreType.DMA
    vmem = pl.BlockSpec(memory_space=pltpu.VMEM)
    hbm = pl.BlockSpec(memory_space=pl.ANY)
    group = pltpu.VMEM((n_tm, CH, LAGS), F32)
    share = pltpu.VMEM((CH, LAGS), F32)
    return pl.pallas_call(
        functools.partial(kernel, n_pairs, n_tm, 1.0 / math.sqrt(2.0 * bins * n_tm)),
        out_shape=jax.ShapeDtypeStruct((TILE_CAP, CH, LAGS), F32),
        in_specs=[hbm] * 5,
        out_specs=vmem,
        scratch_shapes=[
            pltpu.SMEM(channel_slot.shape, jnp.int32),
            pltpu.SMEM(tile_list.shape[::-1], jnp.int32),
            pltpu.SMEM(tile_owner.shape, jnp.int32),
            [pltpu.VMEM((CH, 2, STEP), BF16) for _ in range(steps)],
            pltpu.VMEM((2 * CH, bins), BF16),
            pltpu.VMEM((2 * CH, bins), BF16),
            pltpu.VMEM((bins, LAGS), BF16),
            pltpu.VMEM((2 * CH * CH, LAGS), F32),
            pltpu.VMEM((2 * CH * CH, LAGS), F32),
            group,
            pltpu.VMEM((n_tm - 1, CH, LAGS), F32),
            share,
            share,
            group,
            pltpu.VMEM((2 * n_tm, CH, LAGS), F32),
            pltpu.VMEM((TILE_CAP, CH, LAGS), F32),
            dma((3,)),
            dma((steps,)),
            dma((steps,)),
            dma((1,)),
            dma((steps - 1 + STEP // PIECE,)),
            dma((1,)),
            dma((1,)),
            dma((1,)),
            dma((1,)),
            dma((1,)),
            dma((1,)),
            dma((1,)),
            pltpu.SemaphoreType.REGULAR((3,)),
        ],
        compiler_params=pltpu.CompilerParams(
            collective_id=0, has_side_effects=True, vmem_limit_bytes=48 * 1024 * 1024
        ),
    )(
        *(
            pltpu.with_memory_space_constraint(operand, pltpu.HBM)
            for operand in (
                spectra[0], channel_slot, tile_list.T, tile_owner, jnp.asarray(lag_table(bins))
            )
        )
    )


def solution(mesh):
    placed = (P("tm", "pairs", None, None), P("pairs"), P(), P())
    body = functools.partial(on_device, mesh.shape["pairs"], mesh.shape["tm"])
    return jax.shard_map(
        body, mesh=mesh, in_specs=placed, out_specs=P("pairs", "tm", None), check_vma=False
    )
```

```python
import functools
import math

import jax
import jax.numpy as jnp
import ml_dtypes
import numpy as np
from jax import lax
from jax.experimental import pallas as pl
from jax.experimental.pallas import tpu as pltpu
from jax.sharding import PartitionSpec as P

LAGS = 256
TILE_CAP = 4
CH = 8
HALF = LAGS // 2
TURN = 512
SHIFT = TURN // 4
STEP = 4096
PIECES = ((0, 2048), (2048, 1024), (3072, 512), (3584, 512))
MESH = pl.DeviceIdType.MESH
F32 = jnp.float32
BF16 = jnp.bfloat16


def lag_table(bins):
    bin_ids = np.arange(bins)
    turn_start = bin_ids // TURN * TURN
    moved = turn_start + (bin_ids - turn_start + SHIFT) % TURN

    def phase(ids, lags):
        steps = (ids[:, None] * lags[None, :]) % (2 * bins)
        return (steps.astype(np.float32) * np.float32(math.pi / bins)).astype(np.float64)

    cosine = np.cos(phase(bin_ids, np.arange(HALF)))
    sine = -np.sin(phase(moved, np.arange(HALF)))
    sine[:, :1] = np.cos(phase(bin_ids, np.array([HALF])))
    joined = np.concatenate([cosine, sine], axis=1)
    return joined.astype(np.float32).astype(ml_dtypes.bfloat16)


def moved_on(block):
    parts = []
    for start in range(0, block.shape[1], TURN):
        parts.append(block[:, start + SHIFT : start + TURN])
        parts.append(block[:, start : start + SHIFT])
    return jnp.concatenate(parts, axis=1)


def cross_rows(lead, tail):
    lead = lead.astype(F32)
    tail = tail.astype(F32)
    tail_re, tail_im = tail[:CH], tail[CH:]
    real, imag = [], []
    for a in range(CH):
        lead_re, lead_im = lead[a : a + 1], lead[CH + a : CH + a + 1]
        real.append(lead_re * tail_re + lead_im * tail_im)
        imag.append(lead_im * tail_re - lead_re * tail_im)
    real = jnp.concatenate(real, axis=0).astype(BF16)
    imag = jnp.concatenate(imag, axis=0).astype(BF16)
    return jnp.concatenate([real, moved_on(imag)], axis=0)


def folded(acc):
    real, imag = acc[: CH * CH, :], acc[CH * CH :, :]
    lane = lax.broadcasted_iota(jnp.int32, (CH * CH, HALF), 1)
    right = imag[:, HALF:] + jnp.where(lane == 0, real[:, HALF:], 0.0)
    return jnp.concatenate([real[:, :HALF], right], axis=1)


def kernel(
    n_pairs, n_tm, norm_scale,
    spectra, slot_hbm, tiles_hbm, owners_hbm, table_hbm,
    out,
    slot, tiles, owners, raw, own, beside, table,
    diag_acc, side_acc, diag_out, diag_in, hop_out, hop_in,
    side_out, arrived, mixed,
    index_sem, raw_sem, table_sem, send_sem, recv_sem, diag_send, diag_recv,
    hop_send, hop_recv, own_send, near_send, arrived_sem, ready,
):
    bins = own.shape[1]
    steps = bins // STEP
    here = lax.axis_index("pairs")
    window = lax.axis_index("tm")
    odd = 1 - lax.rem(window, 2)
    even_window = odd == 0
    right = lax.rem(here + 1, n_pairs)
    left = lax.rem(here + n_pairs - 1, n_pairs)
    near = lax.rem(here + 1 - 2 * odd + n_pairs, n_pairs)
    away = lax.rem(here - 1 + 2 * odd + n_pairs, n_pairs)
    to_right = lax.min(n_pairs - 1 - here, 1)
    to_left = lax.min(here, 1)
    has_right = to_right == 1
    has_left = to_left == 1
    to_near = to_right * (1 - odd) + to_left * odd
    to_away = to_left * (1 - odd) + to_right * odd
    has_near = to_near == 1
    has_away = to_away == 1
    gives_own = has_left
    gives_near = has_near & (here * odd != 1)

    def peer(k):
        return lax.rem(window + k, n_tm)

    barrier = pltpu.get_barrier_semaphore()

    def greet(block, t):
        pl.semaphore_signal(barrier, inc=1, device_id=(block, t), device_id_type=MESH)

    @pl.when(has_near)
    def _():
        greet(near, window)

    core = lax.rem(window, 2)
    partner = window + 1 - 2 * core
    beside_odd = [lax.rem(window - core + 2 * dx + n_tm, n_tm) + 1 for dx in (-1, 1)]
    far_first = sorted(range(1, n_tm), key=lambda k: abs(k - n_tm // 2))
    greet(here, partner)

    @pl.when(core == 1)
    def _():
        for t in beside_odd:
            greet(here, t)

    def vouch(place, t):
        pl.semaphore_signal(
            ready.at[place], inc=1, device_id=(here, t), device_id_type=MESH
        )

    def lanes(index):
        return pl.ds(pl.multiple_of(index * STEP, STEP), STEP)

    def raw_copy(part):
        return pltpu.make_async_copy(
            spectra.at[:, :, lanes(part)], raw[part], raw_sem.at[part]
        )

    def table_copy(part):
        return pltpu.make_async_copy(
            table_hbm.at[lanes(part), :], table.at[lanes(part), :], table_sem.at[part]
        )

    index_copies = [
        pltpu.make_async_copy(source, target, index_sem.at[place])
        for place, (source, target) in enumerate(
            [(slot_hbm, slot), (tiles_hbm, tiles), (owners_hbm, owners)]
        )
    ]
    index_copies[0].start()
    for part in range(steps):
        raw_copy(part).start()
    for copy in index_copies[1:]:
        copy.start()
    def block_copy(span, place):
        return pltpu.make_async_remote_copy(
            own.at[:, span], beside.at[:, span], send_sem.at[0], recv_sem.at[place],
            device_id=(away, window), device_id_type=MESH,
        )

    last = [
        (pl.ds((steps - 1) * STEP + start, size), steps - 1 + i)
        for i, (start, size) in enumerate(PIECES)
    ]

    def slot_kinds():
        for copy in index_copies[1:]:
            copy.wait()

        def next_tile(p, carry):
            count, kinds = carry[0], carry[1:]
            mine = owners[p] == here
            kind = 2 * (tiles[0, p] - here + 1) + tiles[1, p] - tiles[0, p]
            kinds = [
                jnp.where(mine & (count == s), kind, kinds[s]) for s in range(TILE_CAP)
            ]
            return (count + mine.astype(jnp.int32), *kinds)

        carry = (jnp.int32(0),) + (jnp.int32(-1),) * TILE_CAP
        return lax.fori_loop(0, tiles.shape[1], next_tile, carry)[1:]

    index_copies[0].wait()
    rows = [slot[c] for c in range(CH)]
    entered = 0
    for part in range(steps):
        if part <= entered:
            raw_copy(part).wait()

        @pl.loop(0, STEP // 1024)
        def _(piece, part=part):
            offset = pl.multiple_of(piece * 1024, 1024)
            values = [raw[part][row, :, pl.ds(offset, 1024)].astype(F32) for row in rows]
            planar = [v[:1] for v in values] + [v[1:] for v in values]
            own[:, pl.ds(pl.multiple_of(part * STEP + offset, 1024), 1024)] = jnp.concatenate(
                planar, axis=0
            ).astype(BF16)

        if part == entered:
            pl.semaphore_wait(barrier, 1 + 2 * core + to_away)

            @pl.when(core == 1)
            def _():
                for t in beside_odd:
                    vouch(0, t)

        if entered <= part < steps - 1:

            @pl.when(has_away)
            def _(part=part):
                for sent in range(0 if part == entered else part, part + 1):
                    block_copy(lanes(sent), sent).start()

        if part == entered:
            for later in range(entered + 1, steps):
                raw_copy(later).wait()
            for later in range(steps):
                table_copy(later).start()

    @pl.when(core == 1)
    def _():
        pl.semaphore_wait(ready.at[0], 2)
        vouch(1, beside_odd[0])

    diag_acc[...] = jnp.zeros_like(diag_acc)
    side_acc[...] = jnp.zeros_like(side_acc)

    @pl.loop(0, steps)
    def _(part):
        table_copy(part).wait()
        block = own[:, lanes(part)]
        diag_acc[...] += jnp.dot(
            cross_rows(block, block), table[lanes(part), :], preferred_element_type=F32
        )

    @pl.when(core == 1)
    def _():
        pl.semaphore_wait(ready.at[1], 1)
        vouch(2, partner)

    @pl.when(core == 0)
    def _():
        pl.semaphore_wait(ready.at[2], 1)

    @pl.when(has_away)
    def _():
        for span, place in last:
            block_copy(span, place).start()

    def diag_copy(k):
        return pltpu.make_async_remote_copy(
            diag_out.at[peer(k)], diag_in.at[k - 1], diag_send.at[0], diag_recv.at[0],
            device_id=(here, peer(k)), device_id_type=MESH,
        )

    diag_all = pltpu.make_async_remote_copy(
        diag_out.at[pl.ds(0, n_tm - 1)], diag_in, diag_send.at[0], diag_recv.at[0],
        device_id=(here, peer(1)), device_id_type=MESH,
    )
    diag = folded(diag_acc[...])
    for t in range(n_tm):
        diag_out[t] = diag[t * CH : (t + 1) * CH]
    for k in far_first:
        diag_copy(k).start()

    kinds = slot_kinds()

    def chosen(s, kind, tile):
        return jnp.where(kinds[s] == kind, tile, 0.0)

    def side_step(span, place):
        block_copy(span, place).wait_recv()
        mine = own[:, span].astype(F32)
        other = beside[:, span].astype(F32)
        lead = jnp.where(even_window, mine, other)
        tail = jnp.where(even_window, other, mine)
        side_acc[...] += jnp.dot(
            cross_rows(lead, tail), table[span, :], preferred_element_type=F32
        )

    hop = pltpu.make_async_remote_copy(
        hop_out, hop_in, hop_send.at[0], hop_recv.at[0],
        device_id=(right, window), device_id_type=MESH,
    )

    @pl.loop(0, steps - 2)
    def _(part):
        @pl.when(has_near)
        def _():
            side_step(lanes(part), part)

    diag_all.wait_recv()
    diag_sum = diag_out[window]
    for k in range(n_tm - 1):
        diag_sum += diag_in[k]
    hop_out[...] = diag_sum

    @pl.when(has_right)
    def _():
        hop.start()

    @pl.when(has_near)
    def _():
        side_step(lanes(steps - 2), steps - 2)
        for span, place in last:
            side_step(span, place)

    def own_copy(k):
        return pltpu.make_async_remote_copy(
            side_out.at[peer(k)], arrived.at[window], own_send.at[0], arrived_sem.at[0],
            device_id=(here, peer(k)), device_id_type=MESH,
        )

    def right_copy(k):
        return pltpu.make_async_remote_copy(
            side_out.at[peer(k)], arrived.at[n_tm + window // 2],
            near_send.at[0], arrived_sem.at[0],
            device_id=(right, peer(k)), device_id_type=MESH,
        )

    def left_copy(k):
        return pltpu.make_async_remote_copy(
            side_out.at[peer(k)], arrived.at[n_tm + n_tm // 2 + window // 2],
            near_send.at[0], arrived_sem.at[0],
            device_id=(left, peer(k)), device_id_type=MESH,
        )

    def several(buffer, count, send):
        return pltpu.make_async_remote_copy(
            buffer.at[pl.ds(0, count)], buffer.at[pl.ds(0, count)], send, arrived_sem.at[0],
            device_id=(right, window), device_id_type=MESH,
        )

    side = folded(side_acc[...])
    for t in range(n_tm):
        side_out[t] = side[t * CH : (t + 1) * CH]

    @pl.when(gives_near)
    def _():
        @pl.when(even_window)
        def _():
            for k in far_first + [0]:
                right_copy(k).start()

        @pl.when(odd == 1)
        def _():
            for k in far_first + [0]:
                left_copy(k).start()

    @pl.when(gives_own)
    def _():
        for k in far_first:
            own_copy(k).start()

    arrived[window] = side_out[window]
    for s in range(TILE_CAP):
        mixed[s] = chosen(s, 2, diag_sum)

    @pl.when(has_away)
    def _():
        pltpu.make_async_remote_copy(
            own, beside, send_sem.at[0], recv_sem.at[0],
            device_id=(away, window), device_id_type=MESH,
        ).wait_send()

    diag_all.wait_send()

    @pl.when(has_right)
    def _():
        hop.wait_send()

    @pl.when(has_left)
    def _():
        hop.wait_recv()
        for s in range(TILE_CAP):
            mixed[s] += chosen(s, 0, hop_in[...])

    @pl.when(has_left & has_right)
    def _():
        several(arrived, 2 * n_tm - 1, own_send.at[0]).wait_recv()
        after = arrived[1]
        for place in range(3, n_tm, 2):
            after += arrived[place]
        for place in range(n_tm + n_tm // 2, 2 * n_tm):
            after += arrived[place]
        for s in range(TILE_CAP):
            mixed[s] += chosen(s, 3, after)

    @pl.when(has_left & (to_right == 0))
    def _():
        several(arrived, n_tm - 1 + n_tm // 2, own_send.at[0]).wait_recv()

    @pl.when(has_left)
    def _():
        before = arrived[0]
        for place in range(2, n_tm, 2):
            before += arrived[place]
        for place in range(n_tm, n_tm + n_tm // 2):
            before += arrived[place]
        for s in range(TILE_CAP):
            mixed[s] += chosen(s, 1, before)

    lane = lax.broadcasted_iota(jnp.int32, (CH, HALF), 1)
    mirror = lax.rem(HALF - lane, HALF)
    for s in range(TILE_CAP):
        cosine, sine = mixed[s, :, :HALF], mixed[s, :, HALF:]
        before = jnp.where(lane == 0, sine, cosine - sine)
        before = jnp.take_along_axis(before, mirror, axis=1)
        after = jnp.where(lane == 0, cosine, cosine + sine)
        out[s] = jnp.concatenate([before, after], axis=1) * norm_scale

    @pl.when(gives_near)
    def _():
        several(arrived, n_tm, near_send.at[0]).wait_send()

    @pl.when(gives_own)
    def _():
        several(arrived, n_tm - 1, own_send.at[0]).wait_send()


def on_device(n_pairs, n_tm, spectra, channel_slot, tile_list, tile_owner):
    bins = spectra.shape[3]
    steps = bins // STEP
    dma = pltpu.SemaphoreType.DMA
    vmem = pl.BlockSpec(memory_space=pltpu.VMEM)
    hbm = pl.BlockSpec(memory_space=pl.ANY)
    group = pltpu.VMEM((n_tm, CH, LAGS), F32)
    share = pltpu.VMEM((CH, LAGS), F32)
    return pl.pallas_call(
        functools.partial(kernel, n_pairs, n_tm, 1.0 / math.sqrt(2.0 * bins * n_tm)),
        out_shape=jax.ShapeDtypeStruct((TILE_CAP, CH, LAGS), F32),
        in_specs=[hbm] * 5,
        out_specs=vmem,
        scratch_shapes=[
            pltpu.SMEM(channel_slot.shape, jnp.int32),
            pltpu.SMEM(tile_list.shape[::-1], jnp.int32),
            pltpu.SMEM(tile_owner.shape, jnp.int32),
            [pltpu.VMEM((CH, 2, STEP), BF16) for _ in range(steps)],
            pltpu.VMEM((2 * CH, bins), BF16),
            pltpu.VMEM((2 * CH, bins), BF16),
            pltpu.VMEM((bins, LAGS), BF16),
            pltpu.VMEM((2 * CH * CH, LAGS), F32),
            pltpu.VMEM((2 * CH * CH, LAGS), F32),
            group,
            pltpu.VMEM((n_tm - 1, CH, LAGS), F32),
            share,
            share,
            group,
            pltpu.VMEM((2 * n_tm, CH, LAGS), F32),
            pltpu.VMEM((TILE_CAP, CH, LAGS), F32),
            dma((3,)),
            dma((steps,)),
            dma((steps,)),
            dma((1,)),
            dma((steps - 1 + len(PIECES),)),
            dma((1,)),
            dma((1,)),
            dma((1,)),
            dma((1,)),
            dma((1,)),
            dma((1,)),
            dma((1,)),
            pltpu.SemaphoreType.REGULAR((3,)),
        ],
        compiler_params=pltpu.CompilerParams(
            collective_id=0, has_side_effects=True, vmem_limit_bytes=48 * 1024 * 1024
        ),
    )(
        *(
            pltpu.with_memory_space_constraint(operand, pltpu.HBM)
            for operand in (
                spectra[0], channel_slot, tile_list.T, tile_owner, jnp.asarray(lag_table(bins))
            )
        )
    )


def solution(mesh):
    placed = (P("tm", "pairs", None, None), P("pairs"), P(), P())
    body = functools.partial(on_device, mesh.shape["pairs"], mesh.shape["tm"])
    return jax.shard_map(
        body, mesh=mesh, in_specs=placed, out_specs=P("pairs", "tm", None), check_vma=False
    )
```

```python
import functools
import math

import jax
import jax.numpy as jnp
import ml_dtypes
import numpy as np
from jax import lax
from jax.experimental import pallas as pl
from jax.experimental.pallas import tpu as pltpu
from jax.sharding import PartitionSpec as P

LAGS = 256
TILE_CAP = 4
CH = 8
HALF = LAGS // 2
TURN = 512
SHIFT = TURN // 4
STEP = 4096
PIECES = ((0, 2048), (2048, 1024), (3072, 512), (3584, 512))
MESH = pl.DeviceIdType.MESH
F32 = jnp.float32
BF16 = jnp.bfloat16


def lag_table(bins):
    bin_ids = np.arange(bins)
    turn_start = bin_ids // TURN * TURN
    moved = turn_start + (bin_ids - turn_start + SHIFT) % TURN

    def phase(ids, lags):
        steps = (ids[:, None] * lags[None, :]) % (2 * bins)
        return (steps.astype(np.float32) * np.float32(math.pi / bins)).astype(np.float64)

    cosine = np.cos(phase(bin_ids, np.arange(HALF)))
    sine = -np.sin(phase(moved, np.arange(HALF)))
    sine[:, :1] = np.cos(phase(bin_ids, np.array([HALF])))
    joined = np.concatenate([cosine, sine], axis=1)
    return joined.astype(np.float32).astype(ml_dtypes.bfloat16)


def moved_on(block):
    parts = []
    for start in range(0, block.shape[1], TURN):
        parts.append(block[:, start + SHIFT : start + TURN])
        parts.append(block[:, start : start + SHIFT])
    return jnp.concatenate(parts, axis=1)


def cross_rows(lead, tail):
    lead = lead.astype(F32)
    tail = tail.astype(F32)
    tail_re, tail_im = tail[:CH], tail[CH:]
    real, imag = [], []
    for a in range(CH):
        lead_re, lead_im = lead[a : a + 1], lead[CH + a : CH + a + 1]
        real.append(lead_re * tail_re + lead_im * tail_im)
        imag.append(lead_im * tail_re - lead_re * tail_im)
    real = jnp.concatenate(real, axis=0).astype(BF16)
    imag = jnp.concatenate(imag, axis=0).astype(BF16)
    return jnp.concatenate([real, moved_on(imag)], axis=0)


def folded(acc):
    real, imag = acc[: CH * CH, :], acc[CH * CH :, :]
    lane = lax.broadcasted_iota(jnp.int32, (CH * CH, HALF), 1)
    right = imag[:, HALF:] + jnp.where(lane == 0, real[:, HALF:], 0.0)
    return jnp.concatenate([real[:, :HALF], right], axis=1)


def kernel(
    n_pairs, n_tm, norm_scale,
    spectra, slot_hbm, tiles_hbm, owners_hbm, table_hbm,
    out,
    slot, tiles, owners, raw, own, beside, table,
    diag_acc, side_acc, diag_out, diag_in, hop_out, hop_in,
    side_out, arrived, mixed,
    index_sem, raw_sem, table_sem, send_sem, recv_sem, diag_send, diag_recv,
    hop_send, hop_recv, own_send, near_send, arrived_sem, ready,
):
    bins = own.shape[1]
    steps = bins // STEP
    here = lax.axis_index("pairs")
    window = lax.axis_index("tm")
    odd = 1 - lax.rem(window, 2)
    even_window = odd == 0
    right = lax.rem(here + 1, n_pairs)
    left = lax.rem(here + n_pairs - 1, n_pairs)
    near = lax.rem(here + 1 - 2 * odd + n_pairs, n_pairs)
    away = lax.rem(here - 1 + 2 * odd + n_pairs, n_pairs)
    to_right = lax.min(n_pairs - 1 - here, 1)
    to_left = lax.min(here, 1)
    has_right = to_right == 1
    has_left = to_left == 1
    to_near = to_right * (1 - odd) + to_left * odd
    to_away = to_left * (1 - odd) + to_right * odd
    has_near = to_near == 1
    has_away = to_away == 1
    gives_own = has_left
    gives_near = has_near & (here * odd != 1)

    def peer(k):
        return lax.rem(window + k, n_tm)

    barrier = pltpu.get_barrier_semaphore()

    def greet(block, t):
        pl.semaphore_signal(barrier, inc=1, device_id=(block, t), device_id_type=MESH)

    @pl.when(has_near)
    def _():
        greet(near, window)

    core = lax.rem(window, 2)
    partner = window + 1 - 2 * core
    beside_odd = [lax.rem(window - core + 2 * dx + n_tm, n_tm) + 1 for dx in (-1, 1)]
    far_first = sorted(range(1, n_tm), key=lambda k: abs(k - n_tm // 2))
    greet(here, partner)

    @pl.when(core == 1)
    def _():
        for t in beside_odd:
            greet(here, t)

    def vouch(place, t):
        pl.semaphore_signal(
            ready.at[place], inc=1, device_id=(here, t), device_id_type=MESH
        )

    def lanes(index):
        return pl.ds(pl.multiple_of(index * STEP, STEP), STEP)

    def raw_copy(part):
        return pltpu.make_async_copy(
            spectra.at[:, :, lanes(part)], raw[part], raw_sem.at[part]
        )

    def table_copy(part):
        return pltpu.make_async_copy(
            table_hbm.at[lanes(part), :], table.at[lanes(part), :], table_sem.at[part]
        )

    index_copies = [
        pltpu.make_async_copy(source, target, index_sem.at[place])
        for place, (source, target) in enumerate(
            [(slot_hbm, slot), (tiles_hbm, tiles), (owners_hbm, owners)]
        )
    ]
    index_copies[0].start()
    for part in range(steps):
        raw_copy(part).start()
    for copy in index_copies[1:]:
        copy.start()
    def block_copy(span, place):
        return pltpu.make_async_remote_copy(
            own.at[:, span], beside.at[:, span], send_sem.at[0], recv_sem.at[place],
            device_id=(away, window), device_id_type=MESH,
        )

    last = [
        (pl.ds((steps - 1) * STEP + start, size), steps - 1 + i)
        for i, (start, size) in enumerate(PIECES)
    ]

    def slot_kinds():
        for copy in index_copies[1:]:
            copy.wait()

        def next_tile(p, carry):
            count, kinds = carry[0], carry[1:]
            mine = owners[p] == here
            kind = 2 * (tiles[0, p] - here + 1) + tiles[1, p] - tiles[0, p]
            kinds = [
                jnp.where(mine & (count == s), kind, kinds[s]) for s in range(TILE_CAP)
            ]
            return (count + mine.astype(jnp.int32), *kinds)

        carry = (jnp.int32(0),) + (jnp.int32(-1),) * TILE_CAP
        return lax.fori_loop(0, tiles.shape[1], next_tile, carry)[1:]

    index_copies[0].wait()
    rows = [slot[c] for c in range(CH)]
    entered = 0
    for part in range(steps):
        if part <= entered:
            raw_copy(part).wait()

        @pl.loop(0, STEP // 1024)
        def _(piece, part=part):
            offset = pl.multiple_of(piece * 1024, 1024)
            values = [raw[part][row, :, pl.ds(offset, 1024)].astype(F32) for row in rows]
            planar = [v[:1] for v in values] + [v[1:] for v in values]
            own[:, pl.ds(pl.multiple_of(part * STEP + offset, 1024), 1024)] = jnp.concatenate(
                planar, axis=0
            ).astype(BF16)

        if part == entered:
            pl.semaphore_wait(barrier, 1 + 2 * core + to_away)
        if entered <= part < steps - 1:

            @pl.when(has_away)
            def _(part=part):
                for sent in range(0 if part == entered else part, part + 1):
                    block_copy(lanes(sent), sent).start()

        if part == entered:
            @pl.when(core == 1)
            def _():
                for t in beside_odd:
                    vouch(0, t)

            for later in range(entered + 1, steps):
                raw_copy(later).wait()
            for later in range(steps):
                table_copy(later).start()

    @pl.when(core == 1)
    def _():
        pl.semaphore_wait(ready.at[0], 2)
        vouch(1, beside_odd[0])

    diag_acc[...] = jnp.zeros_like(diag_acc)
    side_acc[...] = jnp.zeros_like(side_acc)

    @pl.loop(0, steps)
    def _(part):
        table_copy(part).wait()
        block = own[:, lanes(part)]
        diag_acc[...] += jnp.dot(
            cross_rows(block, block), table[lanes(part), :], preferred_element_type=F32
        )

    @pl.when(core == 1)
    def _():
        pl.semaphore_wait(ready.at[1], 1)
        vouch(2, partner)

    @pl.when(core == 0)
    def _():
        pl.semaphore_wait(ready.at[2], 1)

    @pl.when(has_away)
    def _():
        for span, place in last:
            block_copy(span, place).start()

    def diag_copy(k):
        return pltpu.make_async_remote_copy(
            diag_out.at[peer(k)], diag_in.at[k - 1], diag_send.at[0], diag_recv.at[0],
            device_id=(here, peer(k)), device_id_type=MESH,
        )

    diag_all = pltpu.make_async_remote_copy(
        diag_out.at[pl.ds(0, n_tm - 1)], diag_in, diag_send.at[0], diag_recv.at[0],
        device_id=(here, peer(1)), device_id_type=MESH,
    )
    diag = folded(diag_acc[...])
    for t in range(n_tm):
        diag_out[t] = diag[t * CH : (t + 1) * CH]
    for k in far_first:
        diag_copy(k).start()

    kinds = slot_kinds()

    def chosen(s, kind, tile):
        return jnp.where(kinds[s] == kind, tile, 0.0)

    def side_step(span, place):
        block_copy(span, place).wait_recv()
        mine = own[:, span].astype(F32)
        other = beside[:, span].astype(F32)
        lead = jnp.where(even_window, mine, other)
        tail = jnp.where(even_window, other, mine)
        side_acc[...] += jnp.dot(
            cross_rows(lead, tail), table[span, :], preferred_element_type=F32
        )

    hop = pltpu.make_async_remote_copy(
        hop_out, hop_in, hop_send.at[0], hop_recv.at[0],
        device_id=(right, window), device_id_type=MESH,
    )

    @pl.loop(0, steps - 2)
    def _(part):
        @pl.when(has_near)
        def _():
            side_step(lanes(part), part)

    diag_all.wait_recv()
    diag_sum = diag_out[window]
    for k in range(n_tm - 1):
        diag_sum += diag_in[k]
    hop_out[...] = diag_sum

    @pl.when(has_right)
    def _():
        hop.start()

    @pl.when(has_near)
    def _():
        side_step(lanes(steps - 2), steps - 2)
        for span, place in last:
            side_step(span, place)

    def own_copy(k):
        return pltpu.make_async_remote_copy(
            side_out.at[peer(k)], arrived.at[window], own_send.at[0], arrived_sem.at[0],
            device_id=(here, peer(k)), device_id_type=MESH,
        )

    def right_copy(k):
        return pltpu.make_async_remote_copy(
            side_out.at[peer(k)], arrived.at[n_tm + window // 2],
            near_send.at[0], arrived_sem.at[0],
            device_id=(right, peer(k)), device_id_type=MESH,
        )

    def left_copy(k):
        return pltpu.make_async_remote_copy(
            side_out.at[peer(k)], arrived.at[n_tm + n_tm // 2 + window // 2],
            near_send.at[0], arrived_sem.at[0],
            device_id=(left, peer(k)), device_id_type=MESH,
        )

    def several(buffer, count, send):
        return pltpu.make_async_remote_copy(
            buffer.at[pl.ds(0, count)], buffer.at[pl.ds(0, count)], send, arrived_sem.at[0],
            device_id=(right, window), device_id_type=MESH,
        )

    side = folded(side_acc[...])
    for t in range(n_tm):
        side_out[t] = side[t * CH : (t + 1) * CH]

    @pl.when(gives_near)
    def _():
        @pl.when(even_window)
        def _():
            for k in far_first + [0]:
                right_copy(k).start()

        @pl.when(odd == 1)
        def _():
            for k in far_first + [0]:
                left_copy(k).start()

    @pl.when(gives_own)
    def _():
        for k in far_first:
            own_copy(k).start()

    arrived[window] = side_out[window]
    for s in range(TILE_CAP):
        mixed[s] = chosen(s, 2, diag_sum)

    @pl.when(has_away)
    def _():
        pltpu.make_async_remote_copy(
            own, beside, send_sem.at[0], recv_sem.at[0],
            device_id=(away, window), device_id_type=MESH,
        ).wait_send()

    diag_all.wait_send()

    @pl.when(has_right)
    def _():
        hop.wait_send()

    @pl.when(has_left)
    def _():
        hop.wait_recv()
        for s in range(TILE_CAP):
            mixed[s] += chosen(s, 0, hop_in[...])

    @pl.when(has_left & has_right)
    def _():
        several(arrived, 2 * n_tm - 1, own_send.at[0]).wait_recv()
        after = arrived[1]
        for place in range(3, n_tm, 2):
            after += arrived[place]
        for place in range(n_tm + n_tm // 2, 2 * n_tm):
            after += arrived[place]
        for s in range(TILE_CAP):
            mixed[s] += chosen(s, 3, after)

    @pl.when(has_left & (to_right == 0))
    def _():
        several(arrived, n_tm - 1 + n_tm // 2, own_send.at[0]).wait_recv()

    @pl.when(has_left)
    def _():
        before = arrived[0]
        for place in range(2, n_tm, 2):
            before += arrived[place]
        for place in range(n_tm, n_tm + n_tm // 2):
            before += arrived[place]
        for s in range(TILE_CAP):
            mixed[s] += chosen(s, 1, before)

    lane = lax.broadcasted_iota(jnp.int32, (CH, HALF), 1)
    mirror = lax.rem(HALF - lane, HALF)
    for s in range(TILE_CAP):
        cosine, sine = mixed[s, :, :HALF], mixed[s, :, HALF:]
        before = jnp.where(lane == 0, sine, cosine - sine)
        before = jnp.take_along_axis(before, mirror, axis=1)
        after = jnp.where(lane == 0, cosine, cosine + sine)
        out[s] = jnp.concatenate([before, after], axis=1) * norm_scale

    @pl.when(gives_near)
    def _():
        several(arrived, n_tm, near_send.at[0]).wait_send()

    @pl.when(gives_own)
    def _():
        several(arrived, n_tm - 1, own_send.at[0]).wait_send()


def on_device(n_pairs, n_tm, spectra, channel_slot, tile_list, tile_owner):
    bins = spectra.shape[3]
    steps = bins // STEP
    dma = pltpu.SemaphoreType.DMA
    vmem = pl.BlockSpec(memory_space=pltpu.VMEM)
    hbm = pl.BlockSpec(memory_space=pl.ANY)
    group = pltpu.VMEM((n_tm, CH, LAGS), F32)
    share = pltpu.VMEM((CH, LAGS), F32)
    return pl.pallas_call(
        functools.partial(kernel, n_pairs, n_tm, 1.0 / math.sqrt(2.0 * bins * n_tm)),
        out_shape=jax.ShapeDtypeStruct((TILE_CAP, CH, LAGS), F32),
        in_specs=[hbm] * 5,
        out_specs=vmem,
        scratch_shapes=[
            pltpu.SMEM(channel_slot.shape, jnp.int32),
            pltpu.SMEM(tile_list.shape[::-1], jnp.int32),
            pltpu.SMEM(tile_owner.shape, jnp.int32),
            [pltpu.VMEM((CH, 2, STEP), BF16) for _ in range(steps)],
            pltpu.VMEM((2 * CH, bins), BF16),
            pltpu.VMEM((2 * CH, bins), BF16),
            pltpu.VMEM((bins, LAGS), BF16),
            pltpu.VMEM((2 * CH * CH, LAGS), F32),
            pltpu.VMEM((2 * CH * CH, LAGS), F32),
            group,
            pltpu.VMEM((n_tm - 1, CH, LAGS), F32),
            share,
            share,
            group,
            pltpu.VMEM((2 * n_tm, CH, LAGS), F32),
            pltpu.VMEM((TILE_CAP, CH, LAGS), F32),
            dma((3,)),
            dma((steps,)),
            dma((steps,)),
            dma((1,)),
            dma((steps - 1 + len(PIECES),)),
            dma((1,)),
            dma((1,)),
            dma((1,)),
            dma((1,)),
            dma((1,)),
            dma((1,)),
            dma((1,)),
            pltpu.SemaphoreType.REGULAR((3,)),
        ],
        compiler_params=pltpu.CompilerParams(
            collective_id=0, has_side_effects=True, vmem_limit_bytes=48 * 1024 * 1024
        ),
    )(
        *(
            pltpu.with_memory_space_constraint(operand, pltpu.HBM)
            for operand in (
                spectra[0], channel_slot, tile_list.T, tile_owner, jnp.asarray(lag_table(bins))
            )
        )
    )


def solution(mesh):
    placed = (P("tm", "pairs", None, None), P("pairs"), P(), P())
    body = functools.partial(on_device, mesh.shape["pairs"], mesh.shape["tm"])
    return jax.shard_map(
        body, mesh=mesh, in_specs=placed, out_specs=P("pairs", "tm", None), check_vma=False
    )
```
